512 devices in a mesh: dp: 32 (over z, x), tensor: 16 (over y, core).
Axes of the slice: x: 4, y: 8, z: 8, core: 2. Of those that a mesh axis runs over, the one named last changes fastest.
Arguments:
- x_in: bfloat16 [8192, 8192], P('dp', 'tensor'), may hold values from -6 to 6
- z_in: bfloat16 [8192, 8192], P('dp', 'tensor'), may hold values from -6 to 6
- bc_in: bfloat16 [8192, 1024], P('dp'), may hold values from -6 to 6
- dt_in: bfloat16 [8192, 128], P('dp', 'tensor'), may hold values from -5 to 5
- lengths: int32 [32, 6], P('dp'), may hold values from 1 to 128, 256 in all within a row
- panel_bin: int32 [512], P('dp'), may hold values from 0 to 31, as said below
- panel_slot: int32 [512], P('dp'), may hold values from 0 to 15, as said below
- conv_x: float32 [4, 8192], P(None, 'tensor'), may hold values from -3 to 3
- conv_bc: float32 [4, 1024], replicated, may hold values from -3 to 3
- dt_bias: float32 [128], P('tensor'), may hold values from -7 to -2
- a_log: float32 [128], P('tensor'), may hold values from 0 to 2.5
- dskip: float32 [128], P('tensor'), may hold values from 0.5 to 1.5
- gain: float32 [8192], P('tensor'), may hold values from 0.5 to 1.5
- w_out: bfloat16 [8192, 4096], P('tensor', 'dp'), may hold values from -0.0625 to 0.0625
- dout: bfloat16 [8192, 4096], P(('dp', 'tensor')), may hold values from -24 to 24
Outputs:
- grad_x: bfloat16 [8192, 8192], P('dp', 'tensor')
- grad_z: bfloat16 [8192, 8192], P('dp', 'tensor')
- grad_bc: bfloat16 [8192, 1024], P('dp', 'tensor')
- grad_dt: bfloat16 [8192, 128], P('dp', 'tensor')
- grad_wout: bfloat16 [8192, 4096], P('tensor', 'dp')
- grad_conv_x: float32 [4, 8192], P(None, 'tensor')
- grad_conv_bc: float32 [4, 1024], P(None, 'tensor')
- grad_gain: float32 [8192], P('tensor')
- grad_heads: float32 [3, 128], P(None, 'tensor')
The draws below stay inside these ranges and needn't reach their ends.
Inputs may be any that keep to these rules, and one draw needn't show every extreme that they name: `panel_bin`: each device's 16 panels go to bins with exactly 1 of them to each bin they reach, and every bin receives exactly 16 panels. `panel_slot`: the panels dealt to one bin take the positions 0 to 15 once each. Each bin's lengths sum to 256.
All inputs are finite; a program needn't handle non-finite values.
Results may differ from the reference program's by a relative error of at most 0.02.
Values may be sent and summed in bfloat16 or wider, within the bound.
No kernel may reach another device: no remote copies, remote signals or barrier semaphores. Data moves between devices by JAX's collectives and lax.ppermute only.
A program may use at most 128 MiB of HBM per device.

```python
import math
import jax
import jax.numpy as jnp
import numpy as np
from jax import lax

D = 4096
HEADS = 128
HEAD_DIM = 64
GROUPS = 4
NSTATE = 128
KCONV = 4
SPAN = 128
NPAN = 16
RESP = 6
PANEL = 16
INNER = 8192
L = 256
ALLROWS = 8192
N_DP = 32


def deal_plan(key):
    first, second, third, fourth = jax.random.split(key, 4)
    sources = jax.random.permutation(first, N_DP)
    targets = jax.random.permutation(second, N_DP)
    offsets = jax.random.permutation(third, max(N_DP, NPAN))[:NPAN] % N_DP
    senders = jnp.arange(N_DP)[:, None]
    bins = targets[(sources[senders] + offsets[None, :]) % N_DP]

    def shuffle(item):
        return jax.random.permutation(item, NPAN)
    orders = jax.vmap(shuffle)(jax.random.split(fourth, N_DP))
    column = jnp.broadcast_to(jnp.arange(NPAN)[None, :], (N_DP, NPAN))
    slots = orders[bins, column]
    return (bins.reshape(-1).astype(jnp.int32), slots.reshape(-1).astype(jnp.int32))


def draw_panel_bin(key, part):
    bins, slots = deal_plan(key)
    return bins


def draw_panel_slot(key, part):
    bins, slots = deal_plan(key)
    return slots


def raised(entries, rng, source, target, parts, factor):
    owner, partner = [(jnp.arange(entries.shape[dim]) // (entries.shape[dim] // parts)).reshape([-1 if axis == dim else 1 for axis in range(entries.ndim)]) for dim in (source, target)]
    chosen = jax.random.permutation(rng, parts)[partner]
    strong = (owner == chosen) | (owner == (partner + parts // 2) % parts)
    return jnp.where(strong, factor * entries, entries)


def block_levels(key, dims, cuts, low, largest):
    def one(position, parts):
        heights = jax.random.uniform(jax.random.fold_in(jax.random.fold_in(key, 6), position), (parts,), jnp.float32, low / len(cuts), largest / len(cuts))
        return jnp.repeat(jnp.exp(heights), dims[position] // parts).reshape((-1,) + (1,) * (len(dims) - position - 1))

    factor_of = one(*cuts[0])
    for cut in cuts[1:]:
        factor_of = factor_of * one(*cut)
    return factor_of


def profile(amount, total, most, lean):
    loads = [(1 << 20) // math.isqrt(standing ** lean) + 1 for standing in range(2, amount + 1)]
    surplus, counts = total - most - (amount - 1), [1] * (amount - 1)
    while surplus > 0:
        candidates = [i for i in range(amount - 1) if counts[i] < most]
        pool, remaining = sum([loads[i] for i in candidates]), surplus
        for i in candidates:
            extra = min(most - counts[i], max(1, remaining * loads[i] // pool), surplus)
            counts[i] = counts[i] + extra
            surplus = surplus - extra
    return np.array([most] + counts)


def uneven(stream_key, count, total, limit, skew):
    if count == 2:
        one = jax.random.randint(stream_key, (), max(1, total - limit), min(limit, total - 1) + 1)
        return jnp.stack([one, total - one])
    sizes = jnp.asarray(profile(count, total, limit, skew), jnp.int32)
    pairs = (count - 1) // 2
    donor, taker = sizes[1:1 + 2 * pairs:2], sizes[2:2 + 2 * pairs:2]
    slack = jnp.minimum(donor - 1, limit - taker)
    shifted = jax.random.randint(jax.random.fold_in(stream_key, 1), (pairs,), 0, 1 << 20) % (slack + 1)
    sizes = sizes.at[1:1 + 2 * pairs:2].set(donor - shifted).at[2:2 + 2 * pairs:2].set(taker + shifted)
    return sizes[jax.random.permutation(jax.random.fold_in(stream_key, 2), count)]


def bell_draw(key, dims, deviation, reach, shards=(), kind=jnp.bfloat16):
    drawn = deviation * jax.random.normal(key, dims, jnp.float32)
    if shards:
        drawn = drawn * block_levels(key, dims, shards, -0.22, 0.18)
    return jnp.clip(drawn, -reach, reach).astype(kind)


def noise_with(key, extent, deviation, most, cuts, heavy, kind=jnp.bfloat16):
    values = deviation * jax.random.normal(key, extent, jnp.float32)
    if cuts:
        values = values * block_levels(key, extent, cuts, -0.22, 0.18)
    return jnp.clip(raised(values, jax.random.fold_in(key, 3), *heavy), -most, most).astype(kind)


def setup_inputs(seed: int = 0) -> dict:
    key_list = jax.random.split(jax.random.key(seed), 16)
    x_in = bell_draw(key_list[0], (ALLROWS, INNER), 1.0, 6.0, ((0, 32), (1, 16)))
    z_in = bell_draw(key_list[1], (ALLROWS, INNER), 1.0, 6.0, ((0, 32), (1, 16)))
    bc_in = bell_draw(key_list[2], (ALLROWS, GROUPS * 2 * NSTATE), 1.0, 6.0, ((0, 32),))
    dt_in = bell_draw(key_list[3], (ALLROWS, HEADS), 1.0, 5.0, ((0, 32), (1, 16)))
    lengths = jax.vmap(lambda own: uneven(own, RESP, L, L // 2, 2))(jax.random.split(key_list[4], N_DP)).reshape((N_DP, RESP)).astype(jnp.int32)
    panel_bin = draw_panel_bin(jax.random.fold_in(key_list[15], 71), 0)
    panel_slot = draw_panel_slot(jax.random.fold_in(key_list[15], 71), 0)
    conv_x = bell_draw(key_list[7], (KCONV, INNER), KCONV ** -0.5, 3.0, ((1, 16),), jnp.float32)
    conv_bc = bell_draw(key_list[8], (KCONV, GROUPS * 2 * NSTATE), KCONV ** -0.5, 3.0, (), jnp.float32)
    dt_bias = jnp.clip(-7.0 + 5.0 * jax.random.uniform(key_list[9], (HEADS,), jnp.float32) ** block_levels(key_list[9], (HEADS,), ((0, 16),), -0.2, 0.2), -7.0, -2.0)
    a_log = jnp.clip(2.5 * jax.random.uniform(key_list[10], (HEADS,), jnp.float32) ** block_levels(key_list[10], (HEADS,), ((0, 16),), -0.2, 0.2), 0.0, 2.5)
    dskip = jnp.clip(0.5 + 1.0 * jax.random.uniform(key_list[11], (HEADS,), jnp.float32) ** block_levels(key_list[11], (HEADS,), ((0, 16),), -0.2, 0.2), 0.5, 1.5)
    gain = jnp.clip(1.0 + 0.1 * jax.random.normal(key_list[12], (INNER,), jnp.float32), 0.5, 1.5)
    w_out = bell_draw(key_list[13], (INNER, D), INNER ** -0.5, 0.0625, ((0, 16), (1, 32)))
    dout = noise_with(key_list[14], (ALLROWS, D), 1.0, 24.0, ((0, 512),), (0, 1, 512, 6.0))
    return dict(x_in=x_in, z_in=z_in, bc_in=bc_in, dt_in=dt_in, lengths=lengths, panel_bin=panel_bin, panel_slot=panel_slot, conv_x=conv_x, conv_bc=conv_bc, dt_bias=dt_bias, a_log=a_log, dskip=dskip, gain=gain, w_out=w_out, dout=dout)


highest_precision = lax.Precision.HIGHEST

def segment_ids(lengths_row, total_rows):
    ends = jnp.cumsum(lengths_row).astype(jnp.int32)
    positions = jnp.arange(total_rows, dtype=jnp.int32)
    return lax.optimization_barrier(jnp.sum((positions[:, None] >= ends[None, :]).astype(jnp.int32), axis=1)).astype(jnp.int32)

def conv_silu(raw, taps, segment):
    width = taps.shape[0]
    total = raw * taps[width - 1][None, :]
    for offset in range(1, width):
        moved = jnp.concatenate([jnp.zeros((offset, raw.shape[1]), raw.dtype), raw[:-offset]], axis=0)
        earlier = jnp.concatenate([jnp.full((offset,), -1, jnp.int32), segment[:-offset]], axis=0)
        keep = (earlier == segment).astype(raw.dtype)
        total = total + moved * keep[:, None] * taps[width - 1 - offset][None, :]
    return jax.nn.silu(total)

def ssd_group(values, bmat, cmat, step, rate, skip, segment, block):
    total_rows, heads, head_width = values.shape
    state_width = bmat.shape[1]
    count = total_rows // block
    logdecay = (step * rate[None, :]).reshape(count, block, heads)
    cumulative = jnp.cumsum(logdecay, axis=1)
    seg_blocks = segment.reshape(count, block)
    previous = jnp.concatenate([jnp.full((1,), -1, jnp.int32), seg_blocks[:-1, block - 1]], axis=0)
    lower = jnp.arange(block)[:, None] >= jnp.arange(block)[None, :]

    def advance(state, items):
        xblock, bblock, cblock, sblock, cumblock, segblock, prevseg = items
        same = lower & (segblock[:, None] == segblock[None, :])
        gap = cumblock[:, None, :] - cumblock[None, :, :]
        weights = jnp.where(same[:, :, None], jnp.exp(jnp.minimum(gap, 0.0)), 0.0)
        scores = jnp.dot(cblock, bblock.T, precision=highest_precision)
        mixed = scores[:, :, None] * weights * sblock[None, :, :]
        inner = jnp.einsum('tsh,shp->thp', mixed, xblock, precision=highest_precision)
        carried = (segblock == prevseg).astype(jnp.float32)[:, None] * jnp.exp(cumblock)
        from_state = jnp.einsum('tn,hpn->thp', cblock, state, precision=highest_precision) * carried[:, :, None]
        output = inner + from_state + skip[None, :, None] * xblock
        lastseg = segblock[block - 1]
        keep = (segblock == lastseg).astype(jnp.float32)
        toward = jnp.exp(cumblock[block - 1][None, :] - cumblock) * sblock * keep[:, None]
        kept = (lastseg == prevseg).astype(jnp.float32) * jnp.exp(cumblock[block - 1])
        fresh = jnp.einsum('sh,shp,sn->hpn', toward, xblock, bblock, precision=highest_precision)
        return (kept[:, None, None] * state + fresh, output)
    items = (values.reshape(count, block, heads, head_width), bmat.reshape(count, block, state_width), cmat.reshape(count, block, state_width), step.reshape(count, block, heads), cumulative, seg_blocks, previous)
    start = jnp.zeros((heads, head_width, state_width), jnp.float32)
    final_state, outputs = lax.scan(advance, start, items)
    return outputs.reshape(total_rows, heads, head_width)

def layer_output(xraw, zraw, bcraw, dtraw, conv_x, conv_bc, dt_bias, a_log, dskip, gain, segment):
    total_rows = xraw.shape[0]
    xact = conv_silu(xraw, conv_x, segment)
    bcact = conv_silu(bcraw, conv_bc, segment)
    step = jax.nn.softplus(dtraw + dt_bias[None, :])
    rate = -jnp.exp(a_log)
    per_group = HEADS // GROUPS
    pieces = []
    for group in range(GROUPS):
        head_low = group * per_group
        head_high = head_low + per_group
        values = xact[:, head_low * HEAD_DIM:head_high * HEAD_DIM].reshape(total_rows, per_group, HEAD_DIM)
        anchor = group * 2 * NSTATE
        result = ssd_group(values, bcact[:, anchor:anchor + NSTATE], bcact[:, anchor + NSTATE:anchor + 2 * NSTATE], step[:, head_low:head_high], rate[head_low:head_high], dskip[head_low:head_high], segment, SPAN)
        pieces.append(result.reshape(total_rows, per_group * HEAD_DIM))
    mixed = jnp.concatenate(pieces, axis=1)
    gated = mixed * jax.nn.silu(zraw)
    grouped = gated.reshape(total_rows, GROUPS, INNER // GROUPS)
    inverse = lax.rsqrt(lax.optimization_barrier(jnp.mean(grouped * grouped, axis=2)) + 1e-05)
    return (grouped * inverse[:, :, None]).reshape(total_rows, INNER) * gain[None, :]

def reference(x_in, z_in, bc_in, dt_in, lengths, panel_bin, panel_slot, conv_x, conv_bc, dt_bias, a_log, dskip, gain, w_out, dout):
    scale = 1.0 / math.sqrt(ALLROWS)
    target = (panel_bin * NPAN + panel_slot).astype(jnp.int32)
    source = jnp.zeros((N_DP * NPAN,), jnp.int32).at[target].set(jnp.arange(N_DP * NPAN, dtype=jnp.int32))

    def to_bins(array):
        return array.reshape(N_DP * NPAN, PANEL, array.shape[1])[source].reshape(N_DP, L, array.shape[1])

    def to_arrival(array):
        return array.reshape(N_DP * NPAN, PANEL, array.shape[2])[target].reshape(ALLROWS, array.shape[2])

    def per_bin(totals, items):
        xbin, zbin, bcbin, dtbin, lenbin, doutbin = items
        segment = segment_ids(lenbin, L)

        def forward(xraw, zraw, bcraw, dtraw, taps_x, taps_bc, bias, decay_log, skip, norm_gain):
            return layer_output(xraw, zraw, bcraw, dtraw, taps_x, taps_bc, bias, decay_log, skip, norm_gain, segment)
        normed, pull = jax.vjp(forward, xbin.astype(jnp.float32), zbin.astype(jnp.float32), bcbin.astype(jnp.float32), dtbin.astype(jnp.float32), conv_x, conv_bc, dt_bias, a_log, dskip, gain)
        rounded = normed.astype(jnp.bfloat16)
        dnormed = lax.dot_general(doutbin, w_out, (((1,), (1,)), ((), ())), preferred_element_type=jnp.float32)
        grad_xr, grad_zr, grad_bcr, grad_dtr, grad_cx, grad_cbc, grad_bias, grad_alog, grad_skip, grad_g = pull(dnormed)
        wterm = (jnp.dot(rounded.T, doutbin, preferred_element_type=jnp.float32) * scale).astype(jnp.bfloat16)
        wterm = lax.optimization_barrier(wterm).astype(jnp.float32)
        updated = (totals[0] + wterm, totals[1] + grad_cx, totals[2] + grad_cbc, totals[3] + grad_g, totals[4] + jnp.stack([grad_bias, grad_alog, grad_skip]))
        return (updated, (grad_xr.astype(jnp.bfloat16), grad_zr.astype(jnp.bfloat16), grad_bcr.astype(jnp.bfloat16), grad_dtr.astype(jnp.bfloat16)))
    initial = (jnp.zeros((INNER, D), jnp.float32), jnp.zeros((KCONV, INNER), jnp.float32), jnp.zeros((KCONV, GROUPS * 2 * NSTATE), jnp.float32), jnp.zeros((INNER,), jnp.float32), jnp.zeros((3, HEADS), jnp.float32))
    totals, per_bins = lax.scan(per_bin, initial, (to_bins(x_in), to_bins(z_in), to_bins(bc_in), to_bins(dt_in), lengths, dout.reshape(N_DP, L, D)))
    return (to_arrival(per_bins[0]), to_arrival(per_bins[1]), to_arrival(per_bins[2]), to_arrival(per_bins[3]), totals[0].astype(jnp.bfloat16), totals[1] * scale, totals[2] * scale, totals[3] * scale, totals[4] * scale)
```

```python
import functools
import math

import jax
import jax.numpy as jnp
from jax import lax
from jax.experimental import pallas as pl
from jax.experimental.pallas import tpu as pltpu
from jax.sharding import PartitionSpec as P

GROUPS = 4
DP_INNER = 4
PANEL = 16
LANES = 128
FAR = -1e30

exact = lax.Precision.HIGHEST
f32 = jnp.float32
bf16 = jnp.bfloat16
smem = pl.BlockSpec(memory_space=pltpu.SMEM)
vmem = pl.BlockSpec(memory_space=pltpu.VMEM)


def call(body, outs, ins, scalars=0, cost=1, scratch=(), name=None):
    size = sum(math.prod(o.shape) * o.dtype.itemsize for o in outs)
    size += sum(math.prod(i.shape) * i.dtype.itemsize for i in ins)
    return pl.pallas_call(
        body,
        out_shape=outs,
        in_specs=[smem] * scalars + [vmem] * (len(ins) - scalars),
        out_specs=[vmem] * len(outs),
        scratch_shapes=list(scratch),
        compiler_params=pltpu.CompilerParams(vmem_limit_bytes=48 << 20),
        cost_estimate=pl.CostEstimate(
            flops=int(cost * 1e6), bytes_accessed=size, transcendentals=0
        ),
        name=name,
    )(*ins)


def shaped(shape, dtype):
    return jax.ShapeDtypeStruct(shape, dtype)


def dot_tn(a, b, precision=None):
    return lax.dot_general(
        a, b, (((0,), (0,)), ((), ())), precision=precision, preferred_element_type=f32
    )


def dot_nt(a, b, precision=None):
    return lax.dot_general(
        a, b, (((1,), (1,)), ((), ())), precision=precision, preferred_element_type=f32
    )


def dot_nn(a, b, precision=None):
    return lax.dot_general(
        a, b, (((1,), (0,)), ((), ())), precision=precision, preferred_element_type=f32
    )


def row_ids(shape):
    return lax.broadcasted_iota(jnp.int32, shape, 0)


def lane_ids(shape):
    return lax.broadcasted_iota(jnp.int32, shape, 1)


def starts_of(len_ref, shape):
    rows = row_ids(shape)
    start = jnp.zeros(shape, jnp.int32)
    end = jnp.int32(0)
    for k in range(len_ref.shape[1]):
        end = end + len_ref[0, k]
        start = jnp.where(rows >= end, end, start)
    return start


def seen_mask(len_ref, rows):
    shape = (rows, rows)
    lanes = lane_ids(shape)
    return (lanes <= row_ids(shape)) & (lanes >= starts_of(len_ref, shape))


def keep_masks(len_ref, rows, taps):
    shape = (rows, LANES)
    place = row_ids(shape) - starts_of(len_ref, shape)
    return [None] + [(place >= o).astype(f32)[:, :1] for o in range(1, taps)]


def conv(raw, taps, keeps):
    width = len(keeps)
    total = raw * taps[width - 1 : width]
    for o in range(1, width):
        total = total + pltpu.roll(raw, o, 0) * keeps[o] * taps[width - 1 - o : width - o]
    return total


def conv_back(dpre, raw, taps, keeps):
    width = len(keeps)
    rows = raw.shape[0]
    draw = dpre * taps[width - 1 : width]
    dtaps = {width - 1: jnp.sum(dpre * raw, axis=0, keepdims=True)}
    for o in range(1, width):
        kept = dpre * keeps[o]
        draw = draw + pltpu.roll(kept, rows - o, 0) * taps[width - 1 - o : width - o]
        dtaps[width - 1 - o] = jnp.sum(kept * pltpu.roll(raw, o, 0), axis=0, keepdims=True)
    return draw, [dtaps[k] for k in range(width)]


def head_table(channels, head_width):
    shape = (channels, LANES)
    return (row_ids(shape) // head_width == lane_ids(shape)).astype(f32)


def head_spread(channels, head_width):
    shape = (LANES, channels)
    return (lane_ids(shape) // head_width == row_ids(shape)).astype(f32)


def pack_dout_body(co_ref, dout_ref, *d_refs):
    inner = len(d_refs)
    outer = dout_ref.shape[1] // (LANES * inner)
    for k in range(inner):
        block = lax.rem(co_ref[1] + k, inner)
        for z in range(outer):
            low = pl.multiple_of((z * inner + block) * LANES, LANES)
            d_refs[k][:, z * LANES : (z + 1) * LANES] = dout_ref[:, pl.ds(low, LANES)]


def pack_body(bin_ref, slot_ref, co_ref, x_ref, z_ref, bc_ref, dt_ref, a_ref, zs_ref):
    npan = bin_ref.shape[0]
    channels = x_ref.shape[1]
    pair = bc_ref.shape[1] // GROUPS
    heads = dt_ref.shape[1]
    a_ref[...] = jnp.zeros_like(a_ref)
    zs_ref[...] = jnp.zeros_like(zs_ref)
    group = pl.multiple_of(co_ref[0] * pair, pair)
    shape = (PANEL, LANES)
    for p in range(npan):
        rows = slice(p * PANEL, (p + 1) * PANEL)
        to = pl.ds(pl.multiple_of(bin_ref[p] * PANEL, PANEL), PANEL)
        a_ref[to, 0:channels] = x_ref[rows, :]
        a_ref[to, channels : channels + pair] = bc_ref[rows, pl.ds(group, pair)]
        label = (slot_ref[p] * PANEL + 1 + row_ids(shape)).astype(f32)
        lanes = lane_ids(shape)
        meta = jnp.where(lanes == LANES - 1, label, dt_ref[rows, :])
        a_ref[to, channels + pair : channels + pair + LANES] = meta.astype(bf16)
        zs_ref[to, :] = z_ref[rows, :]


def forward_body(
    width,
    heads,
    len_ref,
    co_ref,
    recv_ref,
    cx_ref,
    cbc_ref,
    bias_ref,
    alog_ref,
    skip_ref,
    pt_ref,
    xraw_ref,
    xpre_ref,
    mixed_ref,
    share_ref,
    bcact_ref,
    scores_ref,
    step_ref,
    slope_ref,
    cum_ref,
    cumt_ref,
):
    rows, channels = xraw_ref.shape
    pair = bcact_ref.shape[1]
    state = pair // 2
    head_width = channels // heads
    slots = recv_ref.shape[0]
    label = recv_ref[:, channels + pair : channels + pair + LANES].astype(f32)[:, LANES - 1 :]
    place = (label == (lane_ids((slots, rows)) + 1).astype(f32)).astype(bf16)
    pt_ref[...] = place
    raw = dot_tn(place, recv_ref[...])
    keeps = keep_masks(len_ref, rows, width)
    xraw = raw[:, :channels]
    xraw_ref[...] = xraw.astype(bf16)
    xpre = conv(xraw, cx_ref[...], keeps)
    xpre_ref[...] = xpre
    xact = xpre * jax.nn.sigmoid(xpre)
    bcraw = raw[:, channels : channels + pair]
    share = share_ref.shape[2] // 2
    for s in range(share_ref.shape[0]):
        tile = bcraw[:, (s // 2) * LANES : (s // 2 + 1) * LANES]
        if s % 2:
            tile = pltpu.roll(tile, share, 1)
        share_ref[s] = jnp.where(lane_ids(tile.shape) < share, tile, 0.0)
    group = pl.multiple_of(co_ref[0] * pair, pair)
    bcpre = conv(bcraw, cbc_ref[:, pl.ds(group, pair)], keeps)
    bcact = (bcpre * jax.nn.sigmoid(bcpre)).astype(bf16)
    bcact_ref[...] = bcact
    scores = dot_nt(bcact[:, state:], bcact[:, :state])
    scores_ref[...] = scores
    mask = seen_mask(len_ref, rows)
    dt = raw[:, channels + pair : channels + pair + LANES] + bias_ref[...]
    real = lane_ids(dt.shape) < heads
    step = jnp.where(real, jnp.maximum(dt, 0.0) + jnp.log1p(jnp.exp(-jnp.abs(dt))), 0.0)
    step_ref[...] = step
    slope_ref[...] = jnp.where(real, jax.nn.sigmoid(dt), 0.0)
    cum = dot_nn(mask.astype(f32), step * -jnp.exp(alog_ref[...]), exact)
    cum_ref[...] = cum
    cumt = jnp.transpose(cum)[: cumt_ref.shape[0]]
    cumt_ref[...] = cumt
    scaled = (xact * dot_nn(step, head_spread(channels, head_width), exact)).astype(bf16)
    skipped = xact * skip_ref[...]
    low = lane_ids((rows, LANES)) < head_width
    for p in range(channels // LANES):
        tile = scaled[:, p * LANES : (p + 1) * LANES]
        total = skipped[:, p * LANES : (p + 1) * LANES]
        for half in range(2):
            h = 2 * p + half
            gap = jnp.where(mask, cum[:, h : h + 1] - cumt[h : h + 1, :], FAR)
            weights = (scores * jnp.exp(jnp.minimum(gap, 0.0))).astype(bf16)
            part = jnp.where(low if half == 0 else ~low, tile, jnp.zeros_like(tile))
            total = total + dot_nn(weights, part)
        mixed_ref[:, p * LANES : (p + 1) * LANES] = total


def gate_body(recv_ref, pt_ref, mixed_ref, zb_ref, gated_ref, sums_ref):
    z = dot_tn(pt_ref[...], recv_ref[...])
    zb_ref[...] = z.astype(bf16)
    gated = mixed_ref[...] * (z * jax.nn.sigmoid(z))
    gated_ref[...] = gated
    ones = jnp.ones((8, gated.shape[1]), f32)
    sums_ref[...] = dot_nt(ones, gated * gated, exact)


def as_column(parts):
    total = parts[0][...]
    for part in parts[1:]:
        total = total + part[...]
    return dot_tn(total, jnp.full((8, LANES), 0.125, f32), exact)


def norm_body(size, gated_ref, gain_ref, *refs):
    parts, (normed_ref, inv_ref) = refs[:-2], refs[-2:]
    inverse = lax.rsqrt(as_column(parts) / size + 1e-05)
    inv_ref[...] = inverse
    normed = gated_ref[...] * inverse[:, :1] * gain_ref[...]
    normed_ref[...] = normed.astype(bf16)


def rows_of(out_ref, k):
    tensor, _, panel, columns = out_ref.shape
    return out_ref[:, k].reshape(tensor * panel, columns)


def dnormed_body(out_ref, w_ref, *p_refs):
    w = jnp.concatenate([w_ref[z] for z in range(w_ref.shape[0])], axis=1)
    for k, p_ref in enumerate(p_refs):
        p_ref[...] = dot_nt(rows_of(out_ref, k), w).astype(p_ref.dtype)


def term_body(scale, out_ref, *refs):
    normed, term_ref = refs[:-1], refs[-1]
    total = None
    for k, normed_ref in enumerate(normed):
        part = dot_tn(normed_ref[...], rows_of(out_ref, k))
        total = part if total is None else total + part
    total = (total * scale).astype(bf16)
    for z in range(term_ref.shape[0]):
        term_ref[z] = total[:, z * LANES : (z + 1) * LANES]


def cross_body(gated_ref, inv_ref, gain_ref, *refs):
    parts, (weighted_ref, dgain_ref, sums_ref) = refs[:-3], refs[-3:]
    dnormed = parts[0][...].astype(f32)
    for part in parts[1:]:
        dnormed = dnormed + part[...].astype(f32)
    gated = gated_ref[...]
    product = dnormed * gated
    dgain_ref[...] = jnp.sum(product * inv_ref[:, :1], axis=0, keepdims=True)
    weighted = dnormed * gain_ref[...]
    weighted_ref[...] = weighted
    ones = jnp.ones((8, gated.shape[1]), f32)
    sums_ref[...] = dot_nt(ones, product * gain_ref[...], exact)


def dz_body(size, weighted_ref, gated_ref, mixed_ref, zb_ref, inv_ref, pt_ref, *refs):
    parts, (dy_ref, back_ref) = refs[:-2], refs[-2:]
    inverse = inv_ref[...]
    factor = (inverse * inverse * inverse * as_column(parts) / size)[:, :1]
    dgated = inverse[:, :1] * weighted_ref[...] - gated_ref[...] * factor
    z = zb_ref[...].astype(f32)
    sig = jax.nn.sigmoid(z)
    dy_ref[...] = dgated * (z * sig)
    dz = dgated * mixed_ref[...] * sig * (1.0 + z * (1.0 - sig))
    back_ref[...] = dot_nn(pt_ref[...], dz.astype(bf16)).astype(bf16)


def backward_body(
    width,
    heads,
    len_ref,
    co_ref,
    dy_ref,
    xpre_ref,
    xraw_ref,
    mixed_ref,
    step_ref,
    slope_ref,
    cum_ref,
    cumt_ref,
    scores_ref,
    bcact_ref,
    cx_ref,
    alog_ref,
    skip_ref,
    gx_ref,
    dcx_ref,
    ddt_ref,
    dheads_ref,
    pieces_ref,
):
    rows, channels = xraw_ref.shape
    pair = bcact_ref.shape[1]
    state = pair // 2
    head_width = channels // heads
    mask = seen_mask(len_ref, rows)
    keeps = keep_masks(len_ref, rows, width)
    xpre = xpre_ref[...]
    sig = jax.nn.sigmoid(xpre)
    xact = xpre * sig
    step = step_ref[...]
    spread = dot_nn(step, head_spread(channels, head_width), exact)
    scaled = (xact * spread).astype(bf16)
    dy = dy_ref[...]
    dyb = dy.astype(bf16)
    cum = cum_ref[...]
    cumt = cumt_ref[...]
    scores = scores_ref[...]
    low = lane_ids((rows, LANES)) < head_width
    dscores = jnp.zeros((rows, rows), f32)
    pieces = []
    for p in range(channels // LANES):
        tile = scaled[:, p * LANES : (p + 1) * LANES]
        dtile = dyb[:, p * LANES : (p + 1) * LANES]
        total = None
        for half in range(2):
            h = 2 * p + half
            gap = jnp.where(mask, cum[:, h : h + 1] - cumt[h : h + 1, :], FAR)
            decay = jnp.exp(jnp.minimum(gap, 0.0))
            weights = (scores * decay).astype(bf16)
            part = jnp.where(low if half == 0 else ~low, dtile, jnp.zeros_like(dtile))
            dscores = dscores + dot_nt(part, tile) * decay
            term = dot_tn(weights, part)
            total = term if total is None else total + term
        pieces.append(total)
    dscaled = jnp.concatenate(pieces, axis=1)
    skip = skip_ref[...]
    table = head_table(channels, head_width)
    inner = mixed_ref[...] - skip * xact
    rowsum = dyb.astype(f32) * inner
    colsum = scaled.astype(f32) * dscaled
    change = dot_nn(rowsum - colsum, table, exact)
    direct = dot_nn(xact * dscaled, table, exact)
    dlog = dot_tn(mask.astype(f32), change, exact)
    rate = -jnp.exp(alog_ref[...])
    ddt = (dlog * rate + direct) * slope_ref[...]
    ddt_ref[...] = ddt
    dskip = dot_nn(
        jnp.broadcast_to(jnp.sum(dy * xact, axis=0, keepdims=True), (8, channels)), table, exact
    )
    dheads_ref[0:1] = jnp.sum(ddt, axis=0, keepdims=True)
    dheads_ref[1:2] = jnp.sum(dlog * step * rate, axis=0, keepdims=True)
    dheads_ref[2:3] = dskip[0:1]
    dpre = (dscaled * spread + skip * dy) * (sig * (1.0 + xpre * (1.0 - sig)))
    draw, dtaps = conv_back(dpre, xraw_ref[...].astype(f32), cx_ref[...], keeps)
    gx_ref[...] = draw.astype(bf16)
    for k in range(width):
        dcx_ref[k : k + 1] = dtaps[k]
    dsb = dscores.astype(bf16)
    dbc = (
        dot_tn(dsb, bcact_ref[:, state:]),
        dot_nn(dsb, bcact_ref[:, :state]),
    )
    share = pieces_ref.shape[2] // 2
    for s in range(pieces_ref.shape[0]):
        low_lane = (s * share) % state
        tile = dbc[s * share // state][:, low_lane // LANES * LANES : (low_lane // LANES + 1) * LANES]
        if low_lane % LANES:
            tile = pltpu.roll(tile, share, 1)
        tile = jnp.where(lane_ids(tile.shape) < share, tile, 0.0)
        pieces_ref[jnp.bitwise_xor(co_ref[2], s)] = tile.astype(bf16)


def share_body(
    width,
    len_ref,
    co_ref,
    share_ref,
    taps_ref,
    gx_ref,
    ddt_ref,
    pt_ref,
    dcx_ref,
    dgain_ref,
    dheads_ref,
    *refs,
):
    parts, back_ref, small_ref = refs[:-2], refs[-2], refs[-1]
    rows = ddt_ref.shape[0]
    channels = gx_ref.shape[1]
    slots = back_ref.shape[0]
    keeps = keep_masks(len_ref, rows, width)
    raw = share_ref[co_ref[2]]
    taps = taps_ref[...]
    pre = conv(raw, taps, keeps)
    sig = jax.nn.sigmoid(pre)
    dact = parts[0][...].astype(f32)
    for part in parts[1:]:
        dact = dact + part[...].astype(f32)
    draw, dtaps = conv_back(dact * (sig * (1.0 + pre * (1.0 - sig))), raw, taps, keeps)
    share = LANES // 2
    meta = draw + pltpu.roll(ddt_ref[...], share, 1)
    place = pt_ref[...]
    back_ref[:, :channels] = dot_nn(place, gx_ref[...]).astype(bf16)
    back_ref[:, channels : channels + LANES] = dot_nn(place, meta.astype(bf16)).astype(bf16)
    small_ref[...] = jnp.zeros_like(small_ref)
    small_ref[0:width] = dcx_ref[...]
    small_ref[width : width + 1] = dgain_ref[...]
    small_ref[width + 1 : width + 4, 0:LANES] = dheads_ref[...]
    for k in range(width):
        row = width + 1 + k % 3
        lane = LANES * (1 + k // 3)
        small_ref[row : row + 1, lane : lane + LANES] = dtaps[k]
    half = channels // 2
    block = jnp.concatenate([small_ref[:, :half], small_ref[:, half:]], axis=0).astype(bf16)
    for k in range(slots // PANEL):
        back_ref[k * PANEL : (k + 1) * PANEL, channels + LANES :] = block


def home_z_body(bin_ref, ret_ref, gz_ref):
    for p in range(bin_ref.shape[0]):
        at = pl.ds(pl.multiple_of(bin_ref[p] * PANEL, PANEL), PANEL)
        gz_ref[p * PANEL : (p + 1) * PANEL] = ret_ref[at]


def home_body(
    scale, heads, bin_ref, ret_ref, gx_ref, gbc_ref, gdt_ref, dcx_ref, dcbc_ref, dgain_ref, dheads_ref
):
    channels = gx_ref.shape[1]
    width = dcx_ref.shape[0]
    share = gbc_ref.shape[1]
    for p in range(bin_ref.shape[0]):
        rows = slice(p * PANEL, (p + 1) * PANEL)
        at = pl.ds(pl.multiple_of(bin_ref[p] * PANEL, PANEL), PANEL)
        gx_ref[rows] = ret_ref[at, :channels]
        meta = ret_ref[at, channels : channels + LANES].astype(f32)
        gbc_ref[rows] = meta[:, :share].astype(bf16)
        gdt_ref[rows] = pltpu.roll(meta, LANES - share, 1)[:, :heads].astype(bf16)
    total = None
    for k in range(ret_ref.shape[0] // PANEL):
        part = ret_ref[k * PANEL : (k + 1) * PANEL, channels + LANES :].astype(f32)
        total = part if total is None else total + part
    total = total * scale
    small = jnp.concatenate([total[:8], total[8:]], axis=1)
    dcx_ref[...] = small[:width]
    dgain_ref[...] = small[width : width + 1]
    dheads_ref[...] = small[width + 1 : width + 4, :heads]
    for k in range(width):
        row = width + 1 + k % 3
        lane = LANES * (1 + k // 3)
        dcbc_ref[k : k + 1] = small[row : row + 1, lane : lane + share]


def per_device(
    x_in,
    z_in,
    bc_in,
    dt_in,
    lengths,
    panel_bin,
    panel_slot,
    conv_x,
    conv_bc,
    dt_bias,
    a_log,
    dskip,
    gain,
    w_out,
    dout,
):
    dp = lax.axis_size("dp")
    tensor = lax.axis_size("tensor")
    inner = DP_INNER
    outer = dp // inner
    t_index = lax.axis_index("tensor")
    x_index = lax.axis_index("dp") % inner
    rows, channels = x_in.shape
    heads = dt_in.shape[1]
    head_width = channels // heads
    width = conv_x.shape[0]
    bc_width = conv_bc.shape[1]
    pair = bc_width // GROUPS
    share = bc_width // tensor
    members = tensor // GROUPS
    group = t_index // members
    local = t_index % members
    slots = dp * PANEL
    size = channels * members
    scale = 1.0 / math.sqrt(rows * dp)
    columns = outer * LANES

    coords = jnp.stack([group, x_index, local]).astype(jnp.int32)
    over_z = [[z * inner + x for z in range(outer)] for x in range(inner)]

    def along_x(block, shift):
        route = []
        for z in range(outer):
            for x in range(inner):
                route.append((z * inner + x, z * inner + (x + shift) % inner))
        return lax.ppermute(block, "dp", route)

    def partner(block, flip):
        return lax.ppermute(block, "tensor", [(t, t ^ flip) for t in range(tensor)])

    def in_group(block):
        return [block] + [partner(block, flip) for flip in range(1, members)]

    d_parts = call(
        pack_dout_body,
        [shaped((dout.shape[0], columns), bf16)] * inner,
        [coords, dout],
        scalars=1,
        name="pack_dout",
    )
    d_own = [d_parts[0]] + [along_x(d_parts[k], k) for k in range(1, inner)]
    out_rows = lax.all_gather(jnp.concatenate(d_own, axis=0), "tensor", axis=0, tiled=True)
    out_rows = out_rows.reshape(tensor, inner, dout.shape[0], columns)
    w_cols = lax.all_gather(
        w_out, "dp", axis=0, tiled=True, axis_index_groups=over_z
    ).reshape(outer, channels, LANES)

    dt_wide = jnp.pad(dt_in.astype(f32), ((0, 0), (0, LANES - heads)))
    first = channels + pair + LANES
    send_a, send_z = call(
        pack_body,
        [shaped((slots, first), bf16), shaped((slots, channels), bf16)],
        [panel_bin, panel_slot, coords, x_in, z_in, bc_in, dt_wide],
        scalars=3,
        name="pack",
    )
    recv_a = lax.all_to_all(send_a, "dp", split_axis=0, concat_axis=0, tiled=True)
    recv_z = lax.all_to_all(send_z, "dp", split_axis=0, concat_axis=0, tiled=True)

    bias_row = jnp.pad(dt_bias, (0, LANES - heads))[None, :]
    alog_row = jnp.pad(a_log, (0, LANES - heads))[None, :]
    skip_row = jnp.repeat(dskip, head_width)[None, :]
    gain_row = gain[None, :]
    share_taps = jnp.pad(
        lax.dynamic_slice_in_dim(conv_bc, t_index * share, share, 1),
        ((0, 0), (0, LANES - share)),
    )

    place, xraw, xpre, mixed, raw_share, bcact, scores, step, slope, cum, cumt = call(
        functools.partial(forward_body, width, heads),
        [
            shaped((slots, rows), bf16),
            shaped((rows, channels), bf16),
            shaped((rows, channels), f32),
            shaped((rows, channels), f32),
            shaped((members, rows, LANES), f32),
            shaped((rows, pair), bf16),
            shaped((rows, rows), f32),
            shaped((rows, LANES), f32),
            shaped((rows, LANES), f32),
            shaped((rows, LANES), f32),
            shaped((8, rows), f32),
        ],
        [lengths, coords, recv_a, conv_x, conv_bc, bias_row, alog_row, skip_row],
        scalars=2,
        cost=4000,
        name="forward",
    )
    zb, gated, squares = call(
        gate_body,
        [
            shaped((rows, channels), bf16),
            shaped((rows, channels), f32),
            shaped((8, rows), f32),
        ],
        [recv_z, place, mixed],
        cost=1000,
        name="gate",
    )
    normed, inverse = call(
        functools.partial(norm_body, size),
        [shaped((rows, channels), bf16), shaped((rows, LANES), f32)],
        [gated, gain_row] + in_group(squares),
        cost=500,
        name="norm",
    )

    partial = call(
        dnormed_body,
        [shaped((rows, channels), f32)] + [shaped((rows, channels), bf16)] * (inner - 1),
        [out_rows, w_cols],
        cost=1200,
        name="dnormed",
    )
    d_terms = [partial[0]] + [along_x(partial[k], -k) for k in range(1, inner)]
    weighted, dgain, crossing = call(
        cross_body,
        [
            shaped((rows, channels), f32),
            shaped((1, channels), f32),
            shaped((8, rows), f32),
        ],
        [gated, inverse, gain_row] + d_terms,
        cost=500,
        name="cross",
    )
    dy, back_z = call(
        functools.partial(dz_body, size),
        [shaped((rows, channels), f32), shaped((slots, channels), bf16)],
        [weighted, gated, mixed, zb, inverse, place] + in_group(crossing),
        cost=1000,
        name="dz",
    )
    home_z = lax.all_to_all(back_z, "dp", split_axis=0, concat_axis=0, tiled=True)

    normed_all = [normed] + [along_x(normed, k) for k in range(1, inner)]
    (term,) = call(
        functools.partial(term_body, scale),
        [shaped((outer, channels, LANES), bf16)],
        [out_rows] + normed_all,
        cost=1200,
        name="term",
    )
    grad_wout = lax.psum_scatter(
        term.reshape(outer * channels, LANES),
        "dp",
        scatter_dimension=0,
        axis_index_groups=over_z,
        tiled=True,
    )

    gx, dcx, ddt, dheads, pieces = call(
        functools.partial(backward_body, width, heads),
        [
            shaped((rows, channels), bf16),
            shaped((width, channels), f32),
            shaped((rows, LANES), f32),
            shaped((3, LANES), f32),
            shaped((members, rows, LANES), bf16),
        ],
        [
            lengths,
            coords,
            dy,
            xpre,
            xraw,
            mixed,
            step,
            slope,
            cum,
            cumt,
            scores,
            bcact,
            conv_x,
            alog_row,
            skip_row,
        ],
        scalars=2,
        cost=6000,
        name="backward",
    )
    parts = [pieces[0]] + [partner(pieces[flip], flip) for flip in range(1, members)]
    (back_a,) = call(
        functools.partial(share_body, width),
        [shaped((slots, channels + LANES + channels // 2), bf16)],
        [
            lengths,
            coords,
            raw_share,
            share_taps,
            gx,
            ddt,
            place,
            dcx,
            dgain,
            dheads,
        ]
        + parts,
        scalars=2,
        cost=1500,
        scratch=[pltpu.VMEM((8, channels), f32)],
        name="share",
    )
    home_a = lax.all_to_all(back_a, "dp", split_axis=0, concat_axis=0, tiled=True)
    (grad_z,) = call(
        home_z_body,
        [shaped((rows, channels), bf16)],
        [panel_bin, home_z],
        scalars=1,
        name="home_z",
    )
    grad_x, grad_bc, grad_dt, grad_cx, grad_cbc, grad_gain, grad_heads = call(
        functools.partial(home_body, scale, heads),
        [
            shaped((rows, channels), bf16),
            shaped((rows, share), bf16),
            shaped((rows, heads), bf16),
            shaped((width, channels), f32),
            shaped((width, share), f32),
            shaped((1, channels), f32),
            shaped((3, heads), f32),
        ],
        [panel_bin, home_a],
        scalars=1,
        name="home",
    )
    return (
        grad_x,
        grad_z,
        grad_bc,
        grad_dt,
        grad_wout,
        grad_cx,
        grad_cbc,
        grad_gain[0],
        grad_heads,
    )


def solution(mesh):
    placed = (
        P("dp", "tensor"),
        P("dp", "tensor"),
        P("dp", None),
        P("dp", "tensor"),
        P("dp", None),
        P("dp"),
        P("dp"),
        P(None, "tensor"),
        P(),
        P("tensor"),
        P("tensor"),
        P("tensor"),
        P("tensor"),
        P("tensor", "dp"),
        P(("dp", "tensor"), None),
    )
    return jax.shard_map(
        per_device,
        mesh=mesh,
        in_specs=placed,
        out_specs=(
            P("dp", "tensor"),
            P("dp", "tensor"),
            P("dp", "tensor"),
            P("dp", "tensor"),
            P("tensor", "dp"),
            P(None, "tensor"),
            P(None, "tensor"),
            P("tensor"),
            P(None, "tensor"),
        ),
        check_vma=False,
    )
```

```python
import functools
import math

import jax
import jax.numpy as jnp
from jax import lax
from jax.experimental import pallas as pl
from jax.experimental.pallas import tpu as pltpu
from jax.sharding import PartitionSpec as P

GROUPS = 4
DP_INNER = 4
CORES = 2
PANEL = 16
LANES = 128
FAR = -1e30

exact = lax.Precision.HIGHEST
f32 = jnp.float32
bf16 = jnp.bfloat16
smem = pl.BlockSpec(memory_space=pltpu.SMEM)
vmem = pl.BlockSpec(memory_space=pltpu.VMEM)


def call(body, outs, ins, scalars=0, cost=1, scratch=(), name=None):
    size = sum(math.prod(o.shape) * o.dtype.itemsize for o in outs)
    size += sum(math.prod(i.shape) * i.dtype.itemsize for i in ins)
    return pl.pallas_call(
        body,
        out_shape=outs,
        in_specs=[smem] * scalars + [vmem] * (len(ins) - scalars),
        out_specs=[vmem] * len(outs),
        scratch_shapes=list(scratch),
        compiler_params=pltpu.CompilerParams(vmem_limit_bytes=16 << 20),
        cost_estimate=pl.CostEstimate(
            flops=int(cost * 1e6), bytes_accessed=size, transcendentals=0
        ),
        name=name,
    )(*ins)


def shaped(shape, dtype):
    return jax.ShapeDtypeStruct(shape, dtype)


def dot_tn(a, b, precision=None):
    return lax.dot_general(
        a, b, (((0,), (0,)), ((), ())), precision=precision, preferred_element_type=f32
    )


def dot_nt(a, b, precision=None):
    return lax.dot_general(
        a, b, (((1,), (1,)), ((), ())), precision=precision, preferred_element_type=f32
    )


def dot_nn(a, b, precision=None):
    return lax.dot_general(
        a, b, (((1,), (0,)), ((), ())), precision=precision, preferred_element_type=f32
    )


def row_ids(shape):
    return lax.broadcasted_iota(jnp.int32, shape, 0)


def lane_ids(shape):
    return lax.broadcasted_iota(jnp.int32, shape, 1)


def starts_of(len_ref, shape):
    rows = row_ids(shape)
    start = jnp.zeros(shape, jnp.int32)
    end = jnp.int32(0)
    for k in range(len_ref.shape[1]):
        end = end + len_ref[0, k]
        start = jnp.where(rows >= end, end, start)
    return start


def seen_mask(len_ref, rows):
    shape = (rows, rows)
    lanes = lane_ids(shape)
    return (lanes <= row_ids(shape)) & (lanes >= starts_of(len_ref, shape))


def keep_masks(len_ref, rows, taps):
    shape = (rows, LANES)
    place = row_ids(shape) - starts_of(len_ref, shape)
    return [None] + [(place >= o).astype(f32)[:, :1] for o in range(1, taps)]


def conv(raw, taps, keeps):
    width = len(keeps)
    total = raw * taps[width - 1 : width]
    for o in range(1, width):
        total = total + pltpu.roll(raw, o, 0) * keeps[o] * taps[width - 1 - o : width - o]
    return total


def conv_back(dpre, raw, taps, keeps):
    width = len(keeps)
    rows = raw.shape[0]
    draw = dpre * taps[width - 1 : width]
    dtaps = {width - 1: jnp.sum(dpre * raw, axis=0, keepdims=True)}
    for o in range(1, width):
        kept = dpre * keeps[o]
        draw = draw + pltpu.roll(kept, rows - o, 0) * taps[width - 1 - o : width - o]
        dtaps[width - 1 - o] = jnp.sum(kept * pltpu.roll(raw, o, 0), axis=0, keepdims=True)
    return draw, [dtaps[k] for k in range(width)]


def head_table(channels, head_width):
    shape = (channels, LANES)
    return (row_ids(shape) // head_width == lane_ids(shape)).astype(f32)


def head_spread(channels, head_width):
    shape = (LANES, channels)
    return (lane_ids(shape) // head_width == row_ids(shape)).astype(f32)


def pack_body(
    bin_ref, slot_ref, co_ref, x_ref, z_ref, bc_ref, dt_ref, dout_ref, a_ref, *d_refs
):
    npan = bin_ref.shape[0]
    channels = x_ref.shape[1]
    pair = bc_ref.shape[1] // GROUPS
    a_ref[...] = jnp.zeros_like(a_ref)
    group = pl.multiple_of(co_ref[0] * pair, pair)
    shape = (PANEL, LANES)
    low, high = 2 * channels, 2 * channels + pair
    for p in range(npan):
        rows = slice(p * PANEL, (p + 1) * PANEL)
        to = pl.ds(pl.multiple_of(bin_ref[p] * PANEL, PANEL), PANEL)
        a_ref[to, 0:channels] = x_ref[rows, :]
        a_ref[to, channels:low] = z_ref[rows, :]
        a_ref[to, low:high] = bc_ref[rows, pl.ds(group, pair)]
        label = (slot_ref[p] * PANEL + 1 + row_ids(shape)).astype(f32)
        meta = jnp.where(lane_ids(shape) == LANES - 1, label, dt_ref[rows, :])
        a_ref[to, high : high + LANES] = meta.astype(bf16)
    inner = len(d_refs)
    outer = dout_ref.shape[1] // (LANES * inner)
    for k in range(inner):
        block = lax.rem(co_ref[1] + k, inner)
        for z in range(outer):
            low = pl.multiple_of((z * inner + block) * LANES, LANES)
            d_refs[k][:, z * LANES : (z + 1) * LANES] = dout_ref[:, pl.ds(low, LANES)]


def forward_body(
    width,
    heads,
    len_ref,
    co_ref,
    recv_ref,
    cx_ref,
    cbc_ref,
    bias_ref,
    alog_ref,
    skip_ref,
    pt_ref,
    xraw_ref,
    xpre_ref,
    mixed_ref,
    share_ref,
    bcact_ref,
    scores_ref,
    step_ref,
    slope_ref,
    cum_ref,
    cumt_ref,
    zb_ref,
    gated_ref,
):
    rows, channels = xraw_ref.shape
    pair = bcact_ref.shape[1]
    state = pair // 2
    head_width = channels // heads
    base = 2 * channels
    slots = recv_ref.shape[0]
    label = recv_ref[:, base + pair : base + pair + LANES].astype(f32)[:, LANES - 1 :]
    place = (label == (lane_ids((slots, rows)) + 1).astype(f32)).astype(bf16)
    pt_ref[...] = place
    raw = dot_tn(place, recv_ref[...])
    keeps = keep_masks(len_ref, rows, width)
    xraw = raw[:, :channels]
    xraw_ref[...] = xraw.astype(bf16)
    xpre = conv(xraw, cx_ref[...], keeps)
    xpre_ref[...] = xpre
    xact = xpre * jax.nn.sigmoid(xpre)
    bcraw = raw[:, base : base + pair]
    share = share_ref.shape[2] // 2
    for s in range(share_ref.shape[0]):
        tile = bcraw[:, (s // 2) * LANES : (s // 2 + 1) * LANES]
        if s % 2:
            tile = pltpu.roll(tile, share, 1)
        share_ref[s] = jnp.where(lane_ids(tile.shape) < share, tile, 0.0)
    group = pl.multiple_of(co_ref[0] * pair, pair)
    bcpre = conv(bcraw, cbc_ref[:, pl.ds(group, pair)], keeps)
    bcact = (bcpre * jax.nn.sigmoid(bcpre)).astype(bf16)
    bcact_ref[...] = bcact
    scores = dot_nt(bcact[:, state:], bcact[:, :state])
    scores_ref[...] = scores
    mask = seen_mask(len_ref, rows)
    dt = raw[:, base + pair : base + pair + LANES] + bias_ref[...]
    real = lane_ids(dt.shape) < heads
    step = jnp.where(real, jnp.maximum(dt, 0.0) + jnp.log1p(jnp.exp(-jnp.abs(dt))), 0.0)
    step_ref[...] = step
    slope_ref[...] = jnp.where(real, jax.nn.sigmoid(dt), 0.0)
    cum = dot_nn(mask.astype(f32), step * -jnp.exp(alog_ref[...]), exact)
    cum_ref[...] = cum
    cumt = jnp.transpose(cum)[: cumt_ref.shape[0]]
    cumt_ref[...] = cumt
    scaled = (xact * dot_nn(step, head_spread(channels, head_width), exact)).astype(bf16)
    skipped = xact * skip_ref[...]
    low = lane_ids((rows, LANES)) < head_width
    for p in range(channels // LANES):
        tile = scaled[:, p * LANES : (p + 1) * LANES]
        total = skipped[:, p * LANES : (p + 1) * LANES]
        for half in range(2):
            h = 2 * p + half
            gap = jnp.where(mask, cum[:, h : h + 1] - cumt[h : h + 1, :], FAR)
            weights = (scores * jnp.exp(jnp.minimum(gap, 0.0))).astype(bf16)
            part = jnp.where(low if half == 0 else ~low, tile, jnp.zeros_like(tile))
            total = total + dot_nn(weights, part)
        mixed_ref[:, p * LANES : (p + 1) * LANES] = total
    z = raw[:, channels:base]
    zb_ref[...] = z.astype(bf16)
    gated_ref[...] = mixed_ref[...] * (z * jax.nn.sigmoid(z))


def as_column(parts):
    total = parts[0][...]
    for part in parts[1:]:
        total = total + part[...]
    eighth = jnp.full((8, LANES), 0.125, f32)
    return dot_tn(total[:8], eighth, exact), dot_tn(total[8:], eighth, exact)


def collect_body(co_ref, *refs):
    blocks, half_ref = refs[:-1], refs[-1]
    count = len(blocks)
    for k, block in enumerate(blocks):
        half_ref[lax.rem(co_ref[3] + count - k, count)] = block[...]


def rows_of(co_ref, mine_ref, other_ref, k):
    mine, other = mine_ref[:, k], other_ref[:, k]
    first = co_ref[4] == 0
    both = jnp.stack([jnp.where(first, mine, other), jnp.where(first, other, mine)], axis=1)
    return both.reshape(-1, both.shape[3])


def dnormed_body(co_ref, mine_ref, other_ref, w_ref, *refs):
    p_refs, rows_ref = refs[:-1], refs[-1]
    w = jnp.concatenate([w_ref[z] for z in range(w_ref.shape[0])], axis=1)
    for k, p_ref in enumerate(p_refs):
        rows = rows_of(co_ref, mine_ref, other_ref, k)
        rows_ref[k] = rows
        p_ref[...] = dot_nt(rows, w).astype(p_ref.dtype)


def term_body(scale, co_ref, rows_ref, *refs):
    count = rows_ref.shape[0]
    normed, terms, total_ref = refs[:count], refs[count:-1], refs[-1]
    total = None
    for k, normed_ref in enumerate(normed):
        part = dot_tn(normed_ref[...], rows_ref[k])
        total = part if total is None else total + part
    total_ref[...] = total * scale
    outer = len(terms)
    for k, term_ref in enumerate(terms):
        block = lax.rem(co_ref[5] + outer - k, outer)
        low = pl.multiple_of(block * LANES, LANES)
        term_ref[...] = total_ref[:, pl.ds(low, LANES)].astype(bf16)


def cross_body(gated_ref, gain_ref, *refs):
    parts, (dnormed_ref, sums_ref) = refs[:-2], refs[-2:]
    dnormed = parts[0][...].astype(f32)
    for part in parts[1:]:
        dnormed = dnormed + part[...].astype(f32)
    dnormed_ref[...] = dnormed
    gated = gated_ref[...]
    ones = jnp.ones((8, gated.shape[1]), f32)
    sums_ref[:8] = dot_nt(ones, gated * gated, exact)
    sums_ref[8:] = dot_nt(ones, dnormed * gated * gain_ref[...], exact)


def dz_body(size, dnormed_ref, gain_ref, gated_ref, mixed_ref, zb_ref, pt_ref, *refs):
    parts, (normed_ref, dgain_ref, dy_ref, back_ref) = refs[:-4], refs[-4:]
    squares, crossing = as_column(parts)
    inverse = lax.rsqrt(squares / size + 1e-05)
    factor = (inverse * inverse * inverse * crossing / size)[:, :1]
    inverse = inverse[:, :1]
    gain = gain_ref[...]
    gated = gated_ref[...]
    dnormed = dnormed_ref[...]
    scaled = gated * inverse
    normed_ref[...] = (scaled * gain).astype(bf16)
    dgain_ref[...] = jnp.sum(dnormed * scaled, axis=0, keepdims=True)
    dgated = inverse * (dnormed * gain) - gated * factor
    z = zb_ref[...].astype(f32)
    sig = jax.nn.sigmoid(z)
    dy_ref[...] = dgated * (z * sig)
    dz = dgated * mixed_ref[...] * sig * (1.0 + z * (1.0 - sig))
    back_ref[...] = dot_nn(pt_ref[...], dz.astype(bf16)).astype(bf16)


def backward_body(
    width,
    heads,
    len_ref,
    co_ref,
    dy_ref,
    xpre_ref,
    xraw_ref,
    mixed_ref,
    step_ref,
    slope_ref,
    cum_ref,
    cumt_ref,
    scores_ref,
    bcact_ref,
    cx_ref,
    alog_ref,
    skip_ref,
    gx_ref,
    dcx_ref,
    ddt_ref,
    dheads_ref,
    pieces_ref,
):
    rows, channels = xraw_ref.shape
    pair = bcact_ref.shape[1]
    state = pair // 2
    head_width = channels // heads
    mask = seen_mask(len_ref, rows)
    keeps = keep_masks(len_ref, rows, width)
    xpre = xpre_ref[...]
    sig = jax.nn.sigmoid(xpre)
    xact = xpre * sig
    step = step_ref[...]
    spread = dot_nn(step, head_spread(channels, head_width), exact)
    scaled = (xact * spread).astype(bf16)
    dy = dy_ref[...]
    dyb = dy.astype(bf16)
    cum = cum_ref[...]
    cumt = cumt_ref[...]
    scores = scores_ref[...]
    low = lane_ids((rows, LANES)) < head_width
    dscores = jnp.zeros((rows, rows), f32)
    pieces = []
    for p in range(channels // LANES):
        tile = scaled[:, p * LANES : (p + 1) * LANES]
        dtile = dyb[:, p * LANES : (p + 1) * LANES]
        total = None
        for half in range(2):
            h = 2 * p + half
            gap = jnp.where(mask, cum[:, h : h + 1] - cumt[h : h + 1, :], FAR)
            decay = jnp.exp(jnp.minimum(gap, 0.0))
            weights = (scores * decay).astype(bf16)
            part = jnp.where(low if half == 0 else ~low, dtile, jnp.zeros_like(dtile))
            dscores = dscores + dot_nt(part, tile) * decay
            term = dot_tn(weights, part)
            total = term if total is None else total + term
        pieces.append(total)
    dscaled = jnp.concatenate(pieces, axis=1)
    skip = skip_ref[...]
    table = head_table(channels, head_width)
    inner = mixed_ref[...] - skip * xact
    rowsum = dyb.astype(f32) * inner
    colsum = scaled.astype(f32) * dscaled
    change = dot_nn(rowsum - colsum, table, exact)
    direct = dot_nn(xact * dscaled, table, exact)
    dlog = dot_tn(mask.astype(f32), change, exact)
    rate = -jnp.exp(alog_ref[...])
    ddt = (dlog * rate + direct) * slope_ref[...]
    ddt_ref[...] = ddt
    dskip = dot_nn(
        jnp.broadcast_to(jnp.sum(dy * xact, axis=0, keepdims=True), (8, channels)), table, exact
    )
    dheads_ref[0:1] = jnp.sum(ddt, axis=0, keepdims=True)
    dheads_ref[1:2] = jnp.sum(dlog * step * rate, axis=0, keepdims=True)
    dheads_ref[2:3] = dskip[0:1]
    dpre = (dscaled * spread + skip * dy) * (sig * (1.0 + xpre * (1.0 - sig)))
    draw, dtaps = conv_back(dpre, xraw_ref[...].astype(f32), cx_ref[...], keeps)
    gx_ref[...] = draw.astype(bf16)
    for k in range(width):
        dcx_ref[k : k + 1] = dtaps[k]
    dsb = dscores.astype(bf16)
    dbc = (
        dot_tn(dsb, bcact_ref[:, state:]),
        dot_nn(dsb, bcact_ref[:, :state]),
    )
    share = pieces_ref.shape[2] // 2
    for s in range(pieces_ref.shape[0]):
        low_lane = (s * share) % state
        tile = dbc[s * share // state][:, low_lane // LANES * LANES : (low_lane // LANES + 1) * LANES]
        if low_lane % LANES:
            tile = pltpu.roll(tile, share, 1)
        tile = jnp.where(lane_ids(tile.shape) < share, tile, 0.0)
        pieces_ref[jnp.bitwise_xor(co_ref[2], s)] = tile.astype(bf16)


def share_body(
    width,
    len_ref,
    co_ref,
    share_ref,
    taps_ref,
    gx_ref,
    ddt_ref,
    pt_ref,
    dcx_ref,
    dgain_ref,
    dheads_ref,
    *refs,
):
    parts, back_ref, small_ref = refs[:-2], refs[-2], refs[-1]
    rows = ddt_ref.shape[0]
    channels = gx_ref.shape[1]
    slots = back_ref.shape[0]
    keeps = keep_masks(len_ref, rows, width)
    raw = share_ref[co_ref[2]]
    taps = taps_ref[...]
    pre = conv(raw, taps, keeps)
    sig = jax.nn.sigmoid(pre)
    dact = parts[0][...].astype(f32)
    for part in parts[1:]:
        dact = dact + part[...].astype(f32)
    draw, dtaps = conv_back(dact * (sig * (1.0 + pre * (1.0 - sig))), raw, taps, keeps)
    share = LANES // 2
    meta = draw + pltpu.roll(ddt_ref[...], share, 1)
    place = pt_ref[...]
    back_ref[:, :channels] = dot_nn(place, gx_ref[...]).astype(bf16)
    back_ref[:, channels : channels + LANES] = dot_nn(place, meta.astype(bf16)).astype(bf16)
    small_ref[...] = jnp.zeros_like(small_ref)
    small_ref[0:width] = dcx_ref[...]
    small_ref[width : width + 1] = dgain_ref[...]
    small_ref[width + 1 : width + 4, 0:LANES] = dheads_ref[...]
    for k in range(width):
        row = width + 1 + k % 3
        lane = LANES * (1 + k // 3)
        small_ref[row : row + 1, lane : lane + LANES] = dtaps[k]
    half = channels // 2
    block = jnp.concatenate([small_ref[:, :half], small_ref[:, half:]], axis=0).astype(bf16)
    for k in range(slots // PANEL):
        back_ref[k * PANEL : (k + 1) * PANEL, channels + LANES :] = block


def home_z_body(bin_ref, ret_ref, gz_ref):
    for p in range(bin_ref.shape[0]):
        at = pl.ds(pl.multiple_of(bin_ref[p] * PANEL, PANEL), PANEL)
        gz_ref[p * PANEL : (p + 1) * PANEL] = ret_ref[at]


def home_body(
    scale, heads, bin_ref, ret_ref, gx_ref, gbc_ref, gdt_ref, dcx_ref, dcbc_ref, dgain_ref, dheads_ref
):
    channels = gx_ref.shape[1]
    width = dcx_ref.shape[0]
    share = gbc_ref.shape[1]
    for p in range(bin_ref.shape[0]):
        rows = slice(p * PANEL, (p + 1) * PANEL)
        at = pl.ds(pl.multiple_of(bin_ref[p] * PANEL, PANEL), PANEL)
        gx_ref[rows] = ret_ref[at, :channels]
        meta = ret_ref[at, channels : channels + LANES].astype(f32)
        gbc_ref[rows] = meta[:, :share].astype(bf16)
        gdt_ref[rows] = pltpu.roll(meta, LANES - share, 1)[:, :heads].astype(bf16)
    total = None
    for k in range(ret_ref.shape[0] // PANEL):
        part = ret_ref[k * PANEL : (k + 1) * PANEL, channels + LANES :].astype(f32)
        total = part if total is None else total + part
    total = total * scale
    small = jnp.concatenate([total[:8], total[8:]], axis=1)
    dcx_ref[...] = small[:width]
    dgain_ref[...] = small[width : width + 1]
    dheads_ref[...] = small[width + 1 : width + 4, :heads]
    for k in range(width):
        row = width + 1 + k % 3
        lane = LANES * (1 + k // 3)
        dcbc_ref[k : k + 1] = small[row : row + 1, lane : lane + share]


def per_device(
    x_in,
    z_in,
    bc_in,
    dt_in,
    lengths,
    panel_bin,
    panel_slot,
    conv_x,
    conv_bc,
    dt_bias,
    a_log,
    dskip,
    gain,
    w_out,
    dout,
):
    dp = lax.axis_size("dp")
    tensor = lax.axis_size("tensor")
    inner = DP_INNER
    outer = dp // inner
    t_index = lax.axis_index("tensor")
    x_index = lax.axis_index("dp") % inner
    rows, channels = x_in.shape
    heads = dt_in.shape[1]
    head_width = channels // heads
    width = conv_x.shape[0]
    bc_width = conv_bc.shape[1]
    pair = bc_width // GROUPS
    share = bc_width // tensor
    members = tensor // GROUPS
    group = t_index // members
    local = t_index % members
    slots = dp * PANEL
    size = channels * members
    scale = 1.0 / math.sqrt(rows * dp)
    columns = outer * LANES

    z_index = lax.axis_index("dp") // inner
    coords = jnp.stack(
        [group, x_index, local, t_index // CORES, t_index % CORES, z_index]
    ).astype(jnp.int32)
    over_z = [[z * inner + x for z in range(outer)] for x in range(inner)]

    def along_x(block, shift):
        route = []
        for z in range(outer):
            for x in range(inner):
                route.append((z * inner + x, z * inner + (x + shift) % inner))
        return lax.ppermute(block, "dp", route)

    def along_z(block, shift):
        route = [(d, (d + shift * inner) % dp) for d in range(dp)]
        return lax.ppermute(block, "dp", route)

    def along_y(block, shift):
        route = [(t, (t + shift * CORES) % tensor) for t in range(tensor)]
        return lax.ppermute(block, "tensor", route)

    def partner(block, flip):
        return lax.ppermute(block, "tensor", [(t, t ^ flip) for t in range(tensor)])

    def in_group(block):
        return [block] + [partner(block, flip) for flip in range(1, members)]

    w_cols = lax.all_gather(
        w_out, "dp", axis=0, tiled=True, axis_index_groups=over_z
    ).reshape(outer, channels, LANES)

    dt_wide = jnp.pad(dt_in.astype(f32), ((0, 0), (0, LANES - heads)))
    packed = call(
        pack_body,
        [shaped((slots, 2 * channels + pair + LANES), bf16)]
        + [shaped((dout.shape[0], columns), bf16)] * inner,
        [panel_bin, panel_slot, coords, x_in, z_in, bc_in, dt_wide, dout],
        scalars=3,
        name="pack",
    )
    send, d_parts = packed[0], packed[1:]
    recv = lax.all_to_all(send, "dp", split_axis=0, concat_axis=0, tiled=True)

    d_own = jnp.stack([d_parts[0]] + [along_x(d_parts[k], k) for k in range(1, inner)])
    ring_y = tensor // CORES
    ups, downs = [d_own], []
    for step in range(1, ring_y // 2 + 1):
        ups.append(along_y(ups[-1], 1))
        if step < ring_y - ring_y // 2:
            downs.append(along_y(downs[-1] if downs else d_own, -1))
    (mine,) = call(
        collect_body,
        [shaped((ring_y,) + d_own.shape, bf16)],
        [coords] + ups + downs[::-1],
        scalars=1,
        name="collect",
    )
    other = partner(mine, 1)

    bias_row = jnp.pad(dt_bias, (0, LANES - heads))[None, :]
    alog_row = jnp.pad(a_log, (0, LANES - heads))[None, :]
    skip_row = jnp.repeat(dskip, head_width)[None, :]
    gain_row = gain[None, :]
    share_taps = jnp.pad(
        lax.dynamic_slice_in_dim(conv_bc, t_index * share, share, 1),
        ((0, 0), (0, LANES - share)),
    )

    (
        place,
        xraw,
        xpre,
        mixed,
        raw_share,
        bcact,
        scores,
        step,
        slope,
        cum,
        cumt,
        zb,
        gated,
    ) = call(
        functools.partial(forward_body, width, heads),
        [
            shaped((slots, rows), bf16),
            shaped((rows, channels), bf16),
            shaped((rows, channels), f32),
            shaped((rows, channels), f32),
            shaped((members, rows, LANES), f32),
            shaped((rows, pair), bf16),
            shaped((rows, rows), f32),
            shaped((rows, LANES), f32),
            shaped((rows, LANES), f32),
            shaped((rows, LANES), f32),
            shaped((8, rows), f32),
            shaped((rows, channels), bf16),
            shaped((rows, channels), f32),
        ],
        [lengths, coords, recv, conv_x, conv_bc, bias_row, alog_row, skip_row],
        scalars=2,
        cost=4000,
        name="forward",
    )

    partial = call(
        dnormed_body,
        [shaped((rows, channels), f32)]
        + [shaped((rows, channels), bf16)] * (inner - 1)
        + [shaped((inner, rows, columns), bf16)],
        [coords, mine, other, w_cols],
        scalars=1,
        cost=1200,
        name="dnormed",
    )
    partial, out_rows = partial[:-1], partial[-1]
    d_terms = [partial[0]] + [along_x(partial[k], -k) for k in range(1, inner)]
    dnormed, sums = call(
        cross_body,
        [shaped((rows, channels), f32), shaped((16, rows), f32)],
        [gated, gain_row] + d_terms,
        cost=500,
        name="cross",
    )
    normed, dgain, dy, back_z = call(
        functools.partial(dz_body, size),
        [
            shaped((rows, channels), bf16),
            shaped((1, channels), f32),
            shaped((rows, channels), f32),
            shaped((slots, channels), bf16),
        ],
        [dnormed, gain_row, gated, mixed, zb, place] + in_group(sums),
        cost=1000,
        name="dz",
    )
    home_z = lax.all_to_all(back_z, "dp", split_axis=0, concat_axis=0, tiled=True)

    normed_all = [normed] + [along_x(normed, k) for k in range(1, inner)]
    terms = call(
        functools.partial(term_body, scale),
        [shaped((channels, LANES), bf16)] * outer,
        [coords, out_rows] + normed_all,
        scalars=1,
        cost=1200,
        scratch=[pltpu.VMEM((channels, columns), f32)],
        name="term",
    )

    def add(moved, term):
        return (moved.astype(f32) + term.astype(f32)).astype(bf16)

    far = outer // 2
    down, up = terms[far], terms[far + 1]
    for k in range(far - 1, 0, -1):
        down = add(along_z(down, -1), terms[k])
    for k in range(far + 2, outer):
        up = add(along_z(up, 1), terms[k])
    grad_wout = (
        along_z(down, -1).astype(f32) + along_z(up, 1).astype(f32) + terms[0].astype(f32)
    ).astype(bf16)

    gx, dcx, ddt, dheads, pieces = call(
        functools.partial(backward_body, width, heads),
        [
            shaped((rows, channels), bf16),
            shaped((width, channels), f32),
            shaped((rows, LANES), f32),
            shaped((3, LANES), f32),
            shaped((members, rows, LANES), bf16),
        ],
        [
            lengths,
            coords,
            dy,
            xpre,
            xraw,
            mixed,
            step,
            slope,
            cum,
            cumt,
            scores,
            bcact,
            conv_x,
            alog_row,
            skip_row,
        ],
        scalars=2,
        cost=6000,
        name="backward",
    )
    parts = [pieces[0]] + [partner(pieces[flip], flip) for flip in range(1, members)]
    (back_a,) = call(
        functools.partial(share_body, width),
        [shaped((slots, channels + LANES + channels // 2), bf16)],
        [
            lengths,
            coords,
            raw_share,
            share_taps,
            gx,
            ddt,
            place,
            dcx,
            dgain,
            dheads,
        ]
        + parts,
        scalars=2,
        cost=1500,
        scratch=[pltpu.VMEM((8, channels), f32)],
        name="share",
    )
    home_a = lax.all_to_all(back_a, "dp", split_axis=0, concat_axis=0, tiled=True)
    (grad_z,) = call(
        home_z_body,
        [shaped((rows, channels), bf16)],
        [panel_bin, home_z],
        scalars=1,
        name="home_z",
    )
    grad_x, grad_bc, grad_dt, grad_cx, grad_cbc, grad_gain, grad_heads = call(
        functools.partial(home_body, scale, heads),
        [
            shaped((rows, channels), bf16),
            shaped((rows, share), bf16),
            shaped((rows, heads), bf16),
            shaped((width, channels), f32),
            shaped((width, share), f32),
            shaped((1, channels), f32),
            shaped((3, heads), f32),
        ],
        [panel_bin, home_a],
        scalars=1,
        name="home",
    )
    return (
        grad_x,
        grad_z,
        grad_bc,
        grad_dt,
        grad_wout,
        grad_cx,
        grad_cbc,
        grad_gain[0],
        grad_heads,
    )


def solution(mesh):
    placed = (
        P("dp", "tensor"),
        P("dp", "tensor"),
        P("dp", None),
        P("dp", "tensor"),
        P("dp", None),
        P("dp"),
        P("dp"),
        P(None, "tensor"),
        P(),
        P("tensor"),
        P("tensor"),
        P("tensor"),
        P("tensor"),
        P("tensor", "dp"),
        P(("dp", "tensor"), None),
    )
    return jax.shard_map(
        per_device,
        mesh=mesh,
        in_specs=placed,
        out_specs=(
            P("dp", "tensor"),
            P("dp", "tensor"),
            P("dp", "tensor"),
            P("dp", "tensor"),
            P("tensor", "dp"),
            P(None, "tensor"),
            P(None, "tensor"),
            P("tensor"),
            P(None, "tensor"),
        ),
        check_vma=False,
    )
```

```python
import functools
import math

import jax
import jax.numpy as jnp
from jax import lax
from jax.experimental import pallas as pl
from jax.experimental.pallas import tpu as pltpu
from jax.sharding import PartitionSpec as P

GROUPS = 4
DP_INNER = 4
PANEL = 16
LANES = 128
FAR = -1e30

exact = lax.Precision.HIGHEST
f32 = jnp.float32
bf16 = jnp.bfloat16
smem = pl.BlockSpec(memory_space=pltpu.SMEM)
vmem = pl.BlockSpec(memory_space=pltpu.VMEM)
anywhere = pl.BlockSpec(memory_space=pl.ANY)


def call(body, outs, ins, scalars=0, fetch=(), cost=1, scratch=(), name=None):
    size = sum(math.prod(o.shape) * o.dtype.itemsize for o in outs)
    size += sum(math.prod(i.shape) * i.dtype.itemsize for i in ins)
    specs = [smem] * scalars + [vmem] * (len(ins) - scalars)
    for k in fetch:
        specs[k] = anywhere
    kept = len(ins) + len(outs) + len(scratch)

    def fetching(*refs):
        args, held, sems = list(refs[:kept]), refs[kept:-1], refs[-1]
        copies = []
        for n, k in enumerate(fetch):
            copies.append(pltpu.make_async_copy(args[k], held[n], sems.at[n]))
            args[k] = held[n]
        for copy in copies:
            copy.start()
        for copy in copies:
            copy.wait()
        body(*args)

    extra = []
    if fetch:
        extra = [pltpu.VMEM(ins[k].shape, ins[k].dtype) for k in fetch]
        extra.append(pltpu.SemaphoreType.DMA((len(fetch),)))
    return pl.pallas_call(
        fetching if fetch else body,
        out_shape=outs,
        in_specs=specs,
        out_specs=[vmem] * len(outs),
        scratch_shapes=list(scratch) + extra,
        compiler_params=pltpu.CompilerParams(vmem_limit_bytes=16 << 20),
        cost_estimate=pl.CostEstimate(
            flops=int(cost * 1e6), bytes_accessed=size, transcendentals=0
        ),
        name=name,
    )(*ins)


def shaped(shape, dtype):
    return jax.ShapeDtypeStruct(shape, dtype)


def dot_tn(a, b, precision=None):
    return lax.dot_general(
        a, b, (((0,), (0,)), ((), ())), precision=precision, preferred_element_type=f32
    )


def dot_nt(a, b, precision=None):
    return lax.dot_general(
        a, b, (((1,), (1,)), ((), ())), precision=precision, preferred_element_type=f32
    )


def dot_nn(a, b, precision=None):
    return lax.dot_general(
        a, b, (((1,), (0,)), ((), ())), precision=precision, preferred_element_type=f32
    )


def row_ids(shape):
    return lax.broadcasted_iota(jnp.int32, shape, 0)


def lane_ids(shape):
    return lax.broadcasted_iota(jnp.int32, shape, 1)


def starts_of(len_ref, shape):
    rows = row_ids(shape)
    start = jnp.zeros(shape, jnp.int32)
    end = jnp.int32(0)
    for k in range(len_ref.shape[1]):
        end = end + len_ref[0, k]
        start = jnp.where(rows >= end, end, start)
    return start


def seen_mask(len_ref, rows):
    shape = (rows, rows)
    lanes = lane_ids(shape)
    return (lanes <= row_ids(shape)) & (lanes >= starts_of(len_ref, shape))


def keep_masks(len_ref, rows, taps):
    shape = (rows, LANES)
    place = row_ids(shape) - starts_of(len_ref, shape)
    return [None] + [(place >= o).astype(f32)[:, :1] for o in range(1, taps)]


def conv(raw, taps, keeps):
    width = len(keeps)
    total = raw * taps[width - 1 : width]
    for o in range(1, width):
        total = total + pltpu.roll(raw, o, 0) * keeps[o] * taps[width - 1 - o : width - o]
    return total


def conv_back(dpre, raw, taps, keeps):
    width = len(keeps)
    rows = raw.shape[0]
    draw = dpre * taps[width - 1 : width]
    dtaps = {width - 1: jnp.sum(dpre * raw, axis=0, keepdims=True)}
    for o in range(1, width):
        kept = dpre * keeps[o]
        draw = draw + pltpu.roll(kept, rows - o, 0) * taps[width - 1 - o : width - o]
        dtaps[width - 1 - o] = jnp.sum(kept * pltpu.roll(raw, o, 0), axis=0, keepdims=True)
    return draw, [dtaps[k] for k in range(width)]


def head_table(channels, head_width):
    shape = (channels, LANES)
    return (row_ids(shape) // head_width == lane_ids(shape)).astype(f32)


def head_spread(channels, head_width):
    shape = (LANES, channels)
    return (lane_ids(shape) // head_width == row_ids(shape)).astype(f32)


def pack_dout_body(inner, co_ref, dout_ref, d_ref):
    rows = dout_ref.shape[0]
    outer = dout_ref.shape[1] // (LANES * inner)
    for z in range(outer):
        block = lax.rem(co_ref[3] + outer - z, outer) * inner * LANES
        low = pl.multiple_of(block, LANES)
        for x in range(inner):
            d_ref[x * rows : (x + 1) * rows, z * LANES : (z + 1) * LANES] = dout_ref[
                :, pl.ds(low + x * LANES, LANES)
            ]


def pack_body(bin_ref, slot_ref, co_ref, x_ref, z_ref, bc_ref, dt_ref, a_ref):
    npan = bin_ref.shape[0]
    channels = x_ref.shape[1]
    heads = dt_ref.shape[1]
    pair = bc_ref.shape[1] // GROUPS
    a_ref[...] = jnp.zeros_like(a_ref)
    group = pl.multiple_of(co_ref[0] * pair, pair)
    shape = (PANEL, LANES)
    low, high = 2 * channels, 2 * channels + pair
    widen = (row_ids((heads, LANES)) == lane_ids((heads, LANES))).astype(bf16)
    wide = dot_nn(dt_ref[...], widen)
    for p in range(npan):
        rows = slice(p * PANEL, (p + 1) * PANEL)
        to = pl.ds(pl.multiple_of(bin_ref[p] * PANEL, PANEL), PANEL)
        a_ref[to, 0:channels] = x_ref[rows, :]
        a_ref[to, channels:low] = z_ref[rows, :]
        a_ref[to, low:high] = bc_ref[rows, pl.ds(group, pair)]
        label = (slot_ref[p] * PANEL + 1 + row_ids(shape)).astype(f32)
        meta = jnp.where(lane_ids(shape) == LANES - 1, label, wide[rows, :])
        a_ref[to, high : high + LANES] = meta.astype(bf16)


def forward_body(
    width,
    heads,
    len_ref,
    co_ref,
    recv_ref,
    cx_ref,
    cbc_ref,
    bias_ref,
    alog_ref,
    skip_ref,
    pt_ref,
    xraw_ref,
    xpre_ref,
    mixed_ref,
    share_ref,
    bcact_ref,
    scores_ref,
    step_ref,
    slope_ref,
    cum_ref,
    cumt_ref,
    zb_ref,
    gated_ref,
):
    rows, channels = xraw_ref.shape
    pair = bcact_ref.shape[1]
    state = pair // 2
    head_width = channels // heads
    base = 2 * channels
    slots = recv_ref.shape[0]
    label = recv_ref[:, base + pair : base + pair + LANES].astype(f32)[:, LANES - 1 :]
    place = (label == (lane_ids((slots, rows)) + 1).astype(f32)).astype(bf16)
    pt_ref[...] = place
    raw = dot_tn(place, recv_ref[...])
    keeps = keep_masks(len_ref, rows, width)
    xraw = raw[:, :channels]
    xraw_ref[...] = xraw.astype(bf16)
    xpre = conv(xraw, cx_ref[...], keeps)
    xpre_ref[...] = xpre
    xact = xpre * jax.nn.sigmoid(xpre)
    bcraw = raw[:, base : base + pair]
    share = share_ref.shape[2] // 2
    for s in range(share_ref.shape[0]):
        tile = bcraw[:, (s // 2) * LANES : (s // 2 + 1) * LANES]
        if s % 2:
            tile = pltpu.roll(tile, share, 1)
        share_ref[s] = jnp.where(lane_ids(tile.shape) < share, tile, 0.0)
    group = pl.multiple_of(co_ref[0] * pair, pair)
    bcpre = conv(bcraw, cbc_ref[:, pl.ds(group, pair)], keeps)
    bcact = (bcpre * jax.nn.sigmoid(bcpre)).astype(bf16)
    bcact_ref[...] = bcact
    scores = dot_nt(bcact[:, state:], bcact[:, :state])
    scores_ref[...] = scores
    mask = seen_mask(len_ref, rows)
    dt = raw[:, base + pair : base + pair + LANES] + bias_ref[...]
    real = lane_ids(dt.shape) < heads
    step = jnp.where(real, jnp.maximum(dt, 0.0) + jnp.log1p(jnp.exp(-jnp.abs(dt))), 0.0)
    step_ref[...] = step
    slope_ref[...] = jnp.where(real, jax.nn.sigmoid(dt), 0.0)
    cum = dot_nn(mask.astype(f32), step * -jnp.exp(alog_ref[...]), exact)
    cum_ref[...] = cum
    cumt = jnp.transpose(cum)[: cumt_ref.shape[0]]
    cumt_ref[...] = cumt
    scaled = (xact * dot_nn(step, head_spread(channels, head_width), exact)).astype(bf16)
    skipped = xact * skip_ref[...]
    low = lane_ids((rows, LANES)) < head_width
    for p in range(channels // LANES):
        tile = scaled[:, p * LANES : (p + 1) * LANES]
        total = skipped[:, p * LANES : (p + 1) * LANES]
        for half in range(2):
            h = 2 * p + half
            gap = jnp.where(mask, cum[:, h : h + 1] - cumt[h : h + 1, :], FAR)
            weights = (scores * jnp.exp(jnp.minimum(gap, 0.0))).astype(bf16)
            part = jnp.where(low if half == 0 else ~low, tile, jnp.zeros_like(tile))
            total = total + dot_nn(weights, part)
        mixed_ref[:, p * LANES : (p + 1) * LANES] = total
    z = raw[:, channels:base]
    zb_ref[...] = z.astype(bf16)
    gated_ref[...] = mixed_ref[...] * (z * jax.nn.sigmoid(z))


def as_column(sums_ref):
    total = sums_ref[:16]
    for k in range(1, sums_ref.shape[0] // 16):
        total = total + sums_ref[16 * k : 16 * (k + 1)]
    eighth = jnp.full((8, LANES), 0.125, f32)
    return dot_tn(total[:8], eighth, exact), dot_tn(total[8:], eighth, exact)


def rows_of(out_ref, k):
    tensor, _, panel, columns = out_ref.shape
    return out_ref[:, k].reshape(tensor * panel, columns)


def dnormed_body(out_ref, *refs):
    blocks, p_ref = refs[:-1], refs[-1]
    w = jnp.concatenate([block[...] for block in blocks], axis=1)
    inner = out_ref.shape[1]
    rows = p_ref.shape[0] // inner
    for k in range(inner):
        p_ref[k * rows : (k + 1) * rows] = dot_nt(rows_of(out_ref, k), w).astype(bf16)


def term_body(scale, out_ref, normed_ref, *terms):
    inner = out_ref.shape[1]
    rows = normed_ref.shape[0] // inner
    total = None
    for k in range(inner):
        part = dot_tn(normed_ref[k * rows : (k + 1) * rows], rows_of(out_ref, k))
        total = part if total is None else total + part
    total = (total * scale).astype(bf16)
    for k, term_ref in enumerate(terms):
        term_ref[...] = total[:, k * LANES : (k + 1) * LANES]


def cross_body(gated_ref, gain_ref, parts_ref, dnormed_ref, sums_ref):
    gated = gated_ref[...]
    rows = gated.shape[0]
    dnormed = parts_ref[:rows].astype(f32)
    for k in range(1, parts_ref.shape[0] // rows):
        dnormed = dnormed + parts_ref[k * rows : (k + 1) * rows].astype(f32)
    dnormed_ref[...] = dnormed
    ones = jnp.ones((8, gated.shape[1]), f32)
    squares = dot_nt(ones, gated * gated, exact)
    crossing = dot_nt(ones, dnormed * gated * gain_ref[...], exact)
    for k in range(sums_ref.shape[0] // 16):
        sums_ref[16 * k : 16 * k + 8] = squares
        sums_ref[16 * k + 8 : 16 * k + 16] = crossing


def dz_body(
    size,
    dnormed_ref,
    gain_ref,
    gated_ref,
    mixed_ref,
    zb_ref,
    sums_ref,
    normed_ref,
    dgain_ref,
    dy_ref,
    dz_ref,
):
    squares, crossing = as_column(sums_ref)
    inverse = lax.rsqrt(squares / size + 1e-05)
    factor = (inverse * inverse * inverse * crossing / size)[:, :1]
    inverse = inverse[:, :1]
    gain = gain_ref[...]
    gated = gated_ref[...]
    dnormed = dnormed_ref[...]
    scaled = gated * inverse
    normed = (scaled * gain).astype(bf16)
    rows = gated.shape[0]
    for k in range(normed_ref.shape[0] // rows):
        normed_ref[k * rows : (k + 1) * rows] = normed
    dgain_ref[...] = jnp.sum(dnormed * scaled, axis=0, keepdims=True)
    dgated = inverse * (dnormed * gain) - gated * factor
    z = zb_ref[...].astype(f32)
    sig = jax.nn.sigmoid(z)
    dy_ref[...] = dgated * (z * sig)
    dz = dgated * mixed_ref[...] * sig * (1.0 + z * (1.0 - sig))
    dz_ref[...] = dz.astype(bf16)


def backward_body(
    width,
    heads,
    len_ref,
    dy_ref,
    xpre_ref,
    xraw_ref,
    mixed_ref,
    step_ref,
    slope_ref,
    cum_ref,
    cumt_ref,
    scores_ref,
    bcact_ref,
    cx_ref,
    alog_ref,
    skip_ref,
    gx_ref,
    dcx_ref,
    ddt_ref,
    dheads_ref,
    pieces_ref,
):
    rows, channels = xraw_ref.shape
    pair = bcact_ref.shape[1]
    state = pair // 2
    head_width = channels // heads
    mask = seen_mask(len_ref, rows)
    keeps = keep_masks(len_ref, rows, width)
    xpre = xpre_ref[...]
    sig = jax.nn.sigmoid(xpre)
    xact = xpre * sig
    step = step_ref[...]
    spread = dot_nn(step, head_spread(channels, head_width), exact)
    scaled = (xact * spread).astype(bf16)
    dy = dy_ref[...]
    dyb = dy.astype(bf16)
    cum = cum_ref[...]
    cumt = cumt_ref[...]
    scores = scores_ref[...]
    low = lane_ids((rows, LANES)) < head_width
    dscores = jnp.zeros((rows, rows), f32)
    pieces = []
    for p in range(channels // LANES):
        tile = scaled[:, p * LANES : (p + 1) * LANES]
        dtile = dyb[:, p * LANES : (p + 1) * LANES]
        total = None
        for half in range(2):
            h = 2 * p + half
            gap = jnp.where(mask, cum[:, h : h + 1] - cumt[h : h + 1, :], FAR)
            decay = jnp.exp(jnp.minimum(gap, 0.0))
            weights = (scores * decay).astype(bf16)
            part = jnp.where(low if half == 0 else ~low, dtile, jnp.zeros_like(dtile))
            dscores = dscores + dot_nt(part, tile) * decay
            term = dot_tn(weights, part)
            total = term if total is None else total + term
        pieces.append(total)
    dscaled = jnp.concatenate(pieces, axis=1)
    skip = skip_ref[...]
    table = head_table(channels, head_width)
    inner = mixed_ref[...] - skip * xact
    rowsum = dyb.astype(f32) * inner
    colsum = scaled.astype(f32) * dscaled
    change = dot_nn(rowsum - colsum, table, exact)
    direct = dot_nn(xact * dscaled, table, exact)
    dlog = dot_tn(mask.astype(f32), change, exact)
    rate = -jnp.exp(alog_ref[...])
    ddt = (dlog * rate + direct) * slope_ref[...]
    ddt_ref[...] = ddt
    dskip = dot_nn(
        jnp.broadcast_to(jnp.sum(dy * xact, axis=0, keepdims=True), (8, channels)), table, exact
    )
    dheads_ref[0:1] = jnp.sum(ddt, axis=0, keepdims=True)
    dheads_ref[1:2] = jnp.sum(dlog * step * rate, axis=0, keepdims=True)
    dheads_ref[2:3] = dskip[0:1]
    dpre = (dscaled * spread + skip * dy) * (sig * (1.0 + xpre * (1.0 - sig)))
    draw, dtaps = conv_back(dpre, xraw_ref[...].astype(f32), cx_ref[...], keeps)
    gx_ref[...] = draw.astype(bf16)
    for k in range(width):
        dcx_ref[k : k + 1] = dtaps[k]
    dsb = dscores.astype(bf16)
    dbc = (
        dot_tn(dsb, bcact_ref[:, state:]),
        dot_nn(dsb, bcact_ref[:, :state]),
    )
    share = pieces_ref.shape[1] // 2
    for s in range(pieces_ref.shape[0] // rows):
        low_lane = (s * share) % state
        tile = dbc[s * share // state][:, low_lane // LANES * LANES : (low_lane // LANES + 1) * LANES]
        if low_lane % LANES:
            tile = pltpu.roll(tile, share, 1)
        tile = jnp.where(lane_ids(tile.shape) < share, tile, 0.0)
        pieces_ref[s * rows : (s + 1) * rows] = tile.astype(bf16)


def share_body(
    width,
    len_ref,
    co_ref,
    share_ref,
    taps_ref,
    gx_ref,
    dz_ref,
    ddt_ref,
    pt_ref,
    dcx_ref,
    dgain_ref,
    dheads_ref,
    parts_ref,
    back_ref,
    small_ref,
):
    rows = ddt_ref.shape[0]
    channels = gx_ref.shape[1]
    slots = back_ref.shape[0]
    keeps = keep_masks(len_ref, rows, width)
    raw = share_ref[co_ref[2]]
    taps = taps_ref[...]
    pre = conv(raw, taps, keeps)
    sig = jax.nn.sigmoid(pre)
    dact = parts_ref[:rows].astype(f32)
    for k in range(1, parts_ref.shape[0] // rows):
        dact = dact + parts_ref[k * rows : (k + 1) * rows].astype(f32)
    draw, dtaps = conv_back(dact * (sig * (1.0 + pre * (1.0 - sig))), raw, taps, keeps)
    share = LANES // 2
    meta = draw + pltpu.roll(ddt_ref[...], share, 1)
    place = pt_ref[...]
    back_ref[:, :channels] = dot_nn(place, gx_ref[...]).astype(bf16)
    back_ref[:, channels : 2 * channels] = dot_nn(place, dz_ref[...]).astype(bf16)
    last = 2 * channels + LANES
    back_ref[:, 2 * channels : last] = dot_nn(place, meta.astype(bf16)).astype(bf16)
    small_ref[...] = jnp.zeros_like(small_ref)
    small_ref[0:width] = dcx_ref[...]
    small_ref[width : width + 1] = dgain_ref[...]
    small_ref[width + 1 : width + 4, 0:LANES] = dheads_ref[...]
    for k in range(width):
        row = width + 1 + k % 3
        lane = LANES * (1 + k // 3)
        small_ref[row : row + 1, lane : lane + LANES] = dtaps[k]
    half = channels // 2
    block = jnp.concatenate([small_ref[:, :half], small_ref[:, half:]], axis=0).astype(bf16)
    for k in range(slots // PANEL):
        back_ref[k * PANEL : (k + 1) * PANEL, last:] = block


def home_body(
    scale,
    heads,
    bin_ref,
    ret_ref,
    gx_ref,
    gz_ref,
    gbc_ref,
    gdt_ref,
    dcx_ref,
    dcbc_ref,
    dgain_ref,
    dheads_ref,
):
    channels = gx_ref.shape[1]
    width = dcx_ref.shape[0]
    share = gbc_ref.shape[1]
    last = 2 * channels + LANES
    for p in range(bin_ref.shape[0]):
        rows = slice(p * PANEL, (p + 1) * PANEL)
        at = pl.ds(pl.multiple_of(bin_ref[p] * PANEL, PANEL), PANEL)
        gx_ref[rows] = ret_ref[at, :channels]
        gz_ref[rows] = ret_ref[at, channels : 2 * channels]
        meta = ret_ref[at, 2 * channels : last].astype(f32)
        gbc_ref[rows] = meta[:, :share].astype(bf16)
        gdt_ref[rows] = pltpu.roll(meta, LANES - share, 1)[:, :heads].astype(bf16)
    total = None
    for k in range(ret_ref.shape[0] // PANEL):
        part = ret_ref[k * PANEL : (k + 1) * PANEL, last:].astype(f32)
        total = part if total is None else total + part
    total = total * scale
    small = jnp.concatenate([total[:8], total[8:]], axis=1)
    dcx_ref[...] = small[:width]
    dgain_ref[...] = small[width : width + 1]
    dheads_ref[...] = small[width + 1 : width + 4, :heads]
    for k in range(width):
        row = width + 1 + k % 3
        lane = LANES * (1 + k // 3)
        dcbc_ref[k : k + 1] = small[row : row + 1, lane : lane + share]


def per_device(
    x_in,
    z_in,
    bc_in,
    dt_in,
    lengths,
    panel_bin,
    panel_slot,
    conv_x,
    conv_bc,
    dt_bias,
    a_log,
    dskip,
    gain,
    w_out,
    dout,
):
    dp = lax.axis_size("dp")
    tensor = lax.axis_size("tensor")
    inner = DP_INNER
    outer = dp // inner
    t_index = lax.axis_index("tensor")
    x_index = lax.axis_index("dp") % inner
    rows, channels = x_in.shape
    heads = dt_in.shape[1]
    head_width = channels // heads
    width = conv_x.shape[0]
    bc_width = conv_bc.shape[1]
    pair = bc_width // GROUPS
    share = bc_width // tensor
    members = tensor // GROUPS
    group = t_index // members
    local = t_index % members
    slots = dp * PANEL
    size = channels * members
    scale = 1.0 / math.sqrt(rows * dp)
    columns = outer * LANES

    z_index = lax.axis_index("dp") // inner
    coords = jnp.stack([group, x_index, local, z_index]).astype(jnp.int32)
    over_x = [[z * inner + x for x in range(inner)] for z in range(outer)]
    in_group = [[g * members + m for m in range(members)] for g in range(GROUPS)]

    def along_z(block, shift):
        route = [(d, (d + shift * inner) % dp) for d in range(dp)]
        return lax.ppermute(block, "dp", route)

    def swap(blocks, axis, groups=None):
        return lax.all_to_all(
            blocks, axis, split_axis=0, concat_axis=0, tiled=True, axis_index_groups=groups
        )

    (d_parts,) = call(
        functools.partial(pack_dout_body, inner),
        [shaped((inner * dout.shape[0], columns), bf16)],
        [coords, dout],
        scalars=1,
        fetch=(1,),
        name="pack_dout",
    )
    d_own = swap(d_parts, "dp", over_x)
    out_rows = lax.all_gather(d_own, "tensor", axis=0, tiled=True)
    out_rows = out_rows.reshape(tensor, inner, dout.shape[0], columns)

    (send,) = call(
        pack_body,
        [shaped((slots, 2 * channels + pair + LANES), bf16)],
        [panel_bin, panel_slot, coords, x_in, z_in, bc_in, dt_in],
        scalars=3,
        fetch=(3, 4, 5, 6),
        name="pack",
    )
    recv = swap(send, "dp")

    ups, downs = [w_out], [w_out]
    for step in range(1, outer // 2 + 1):
        ups.append(along_z(ups[-1], 1))
        if step < outer - outer // 2:
            downs.append(along_z(downs[-1], -1))
    w_cols = ups + downs[:0:-1]

    bias_row = jnp.pad(dt_bias, (0, LANES - heads))[None, :]
    alog_row = jnp.pad(a_log, (0, LANES - heads))[None, :]
    skip_row = jnp.repeat(dskip, head_width)[None, :]
    gain_row = gain[None, :]
    share_taps = jnp.pad(
        lax.dynamic_slice_in_dim(conv_bc, t_index * share, share, 1),
        ((0, 0), (0, LANES - share)),
    )

    (
        place,
        xraw,
        xpre,
        mixed,
        raw_share,
        bcact,
        scores,
        step,
        slope,
        cum,
        cumt,
        zb,
        gated,
    ) = call(
        functools.partial(forward_body, width, heads),
        [
            shaped((slots, rows), bf16),
            shaped((rows, channels), bf16),
            shaped((rows, channels), f32),
            shaped((rows, channels), f32),
            shaped((members, rows, LANES), f32),
            shaped((rows, pair), bf16),
            shaped((rows, rows), f32),
            shaped((rows, LANES), f32),
            shaped((rows, LANES), f32),
            shaped((rows, LANES), f32),
            shaped((8, rows), f32),
            shaped((rows, channels), bf16),
            shaped((rows, channels), f32),
        ],
        [lengths, coords, recv, conv_x, conv_bc, bias_row, alog_row, skip_row],
        scalars=2,
        fetch=(3, 4, 5, 6, 7),
        cost=4000,
        name="forward",
    )

    (partial,) = call(
        dnormed_body,
        [shaped((inner * rows, channels), bf16)],
        [out_rows] + w_cols,
        fetch=range(outer + 1),
        cost=1200,
        name="dnormed",
    )
    dnormed, sums = call(
        cross_body,
        [shaped((rows, channels), f32), shaped((members * 16, rows), f32)],
        [gated, gain_row, swap(partial, "dp", over_x)],
        cost=500,
        name="cross",
    )
    normed, dgain, dy, dz = call(
        functools.partial(dz_body, size),
        [
            shaped((inner * rows, channels), bf16),
            shaped((1, channels), f32),
            shaped((rows, channels), f32),
            shaped((rows, channels), bf16),
        ],
        [dnormed, gain_row, gated, mixed, zb, swap(sums, "tensor", in_group)],
        cost=1000,
        name="dz",
    )

    gx, dcx, ddt, dheads, pieces = call(
        functools.partial(backward_body, width, heads),
        [
            shaped((rows, channels), bf16),
            shaped((width, channels), f32),
            shaped((rows, LANES), f32),
            shaped((3, LANES), f32),
            shaped((members * rows, LANES), bf16),
        ],
        [
            lengths,
            dy,
            xpre,
            xraw,
            mixed,
            step,
            slope,
            cum,
            cumt,
            scores,
            bcact,
            conv_x,
            alog_row,
            skip_row,
        ],
        scalars=1,
        fetch=range(2, 14),
        cost=6000,
        name="backward",
    )

    terms = call(
        functools.partial(term_body, scale),
        [shaped((channels, LANES), bf16)] * outer,
        [out_rows, swap(normed, "dp", over_x)],
        fetch=(0,),
        cost=1200,
        name="term",
    )
    (back,) = call(
        functools.partial(share_body, width),
        [shaped((slots, 2 * channels + LANES + channels // 2), bf16)],
        [
            lengths,
            coords,
            raw_share,
            share_taps,
            gx,
            dz,
            ddt,
            place,
            dcx,
            dgain,
            dheads,
            swap(pieces, "tensor", in_group),
        ],
        scalars=2,
        fetch=(2, 3, 5, 7, 9),
        cost=1500,
        scratch=[pltpu.VMEM((8, channels), f32)],
        name="share",
    )
    home = swap(back, "dp")

    def add(moved, term):
        return (moved.astype(f32) + term.astype(f32)).astype(bf16)

    far = outer // 2
    down, up = terms[far], terms[far + 1]
    for k in range(far - 1, 0, -1):
        down = add(along_z(down, -1), terms[k])
    for k in range(far + 2, outer):
        up = add(along_z(up, 1), terms[k])
    grad_wout = (
        along_z(down, -1).astype(f32) + along_z(up, 1).astype(f32) + terms[0].astype(f32)
    ).astype(bf16)

    grad_x, grad_z, grad_bc, grad_dt, grad_cx, grad_cbc, grad_gain, grad_heads = call(
        functools.partial(home_body, scale, heads),
        [
            shaped((rows, channels), bf16),
            shaped((rows, channels), bf16),
            shaped((rows, share), bf16),
            shaped((rows, heads), bf16),
            shaped((width, channels), f32),
            shaped((width, share), f32),
            shaped((1, channels), f32),
            shaped((3, heads), f32),
        ],
        [panel_bin, home],
        scalars=1,
        name="home",
    )
    return (
        grad_x,
        grad_z,
        grad_bc,
        grad_dt,
        grad_wout,
        grad_cx,
        grad_cbc,
        grad_gain[0],
        grad_heads,
    )


def solution(mesh):
    placed = (
        P("dp", "tensor"),
        P("dp", "tensor"),
        P("dp", None),
        P("dp", "tensor"),
        P("dp", None),
        P("dp"),
        P("dp"),
        P(None, "tensor"),
        P(),
        P("tensor"),
        P("tensor"),
        P("tensor"),
        P("tensor"),
        P("tensor", "dp"),
        P(("dp", "tensor"), None),
    )
    return jax.shard_map(
        per_device,
        mesh=mesh,
        in_specs=placed,
        out_specs=(
            P("dp", "tensor"),
            P("dp", "tensor"),
            P("dp", "tensor"),
            P("dp", "tensor"),
            P("tensor", "dp"),
            P(None, "tensor"),
            P(None, "tensor"),
            P("tensor"),
            P(None, "tensor"),
        ),
        check_vma=False,
    )
```

```python
import functools
import math

import jax
import jax.numpy as jnp
from jax import lax
from jax.experimental import pallas as pl
from jax.experimental.pallas import tpu as pltpu
from jax.sharding import PartitionSpec as P

GROUPS = 4
DP_INNER = 4
CORES = 2
PANEL = 16
LANES = 128
FAR = -1e30

exact = lax.Precision.HIGHEST
f32 = jnp.float32
bf16 = jnp.bfloat16
smem = pl.BlockSpec(memory_space=pltpu.SMEM)
vmem = pl.BlockSpec(memory_space=pltpu.VMEM)
vmem = pl.BlockSpec(memory_space=pltpu.VMEM)
hbm = pl.BlockSpec(memory_space=pltpu.HBM)


def call(body, outs, ins, scalars=0, moves=False, cost=1, scratch=(), name=None):
    count = len(ins)
    size = sum(math.prod(a.shape) * a.dtype.itemsize for a in list(outs) + list(ins))
    moved = list(ins[scalars:]) + list(outs) if moves else []

    def moving(*refs):
        far, rest = refs[scalars : count + len(outs)], refs[count + len(outs) :]
        held, own, sems = rest[: len(moved)], rest[len(moved) : -1], rest[-1]
        copies = []
        for n in range(len(moved)):
            inward = n < count - scalars
            ends = (far[n], held[n]) if inward else (held[n], far[n])
            copies.append(pltpu.make_async_copy(*ends, sems.at[n]))
        inward, outward = copies[: count - scalars], copies[count - scalars :]
        for copy in inward:
            copy.start()
        for copy in inward:
            copy.wait()
        body(*refs[:scalars], *held, *own)
        for copy in outward:
            copy.start()
        for copy in outward:
            copy.wait()

    place = hbm if moves else vmem
    extra = [pltpu.VMEM(a.shape, a.dtype) for a in moved]
    extra += list(scratch)
    if moves:
        extra.append(pltpu.SemaphoreType.DMA((len(moved),)))
    return pl.pallas_call(
        moving if moves else body,
        out_shape=outs,
        in_specs=[smem] * scalars + [place] * (count - scalars),
        out_specs=[place] * len(outs),
        scratch_shapes=extra,
        compiler_params=pltpu.CompilerParams(vmem_limit_bytes=(58 if moves else 16) << 20),
        cost_estimate=pl.CostEstimate(
            flops=int(cost * 1e6), bytes_accessed=size, transcendentals=0
        ),
        name=name,
    )(*ins)


def shaped(shape, dtype):
    return jax.ShapeDtypeStruct(shape, dtype)


def dot_tn(a, b, precision=None):
    return lax.dot_general(
        a, b, (((0,), (0,)), ((), ())), precision=precision, preferred_element_type=f32
    )


def dot_nt(a, b, precision=None):
    return lax.dot_general(
        a, b, (((1,), (1,)), ((), ())), precision=precision, preferred_element_type=f32
    )


def dot_nn(a, b, precision=None):
    return lax.dot_general(
        a, b, (((1,), (0,)), ((), ())), precision=precision, preferred_element_type=f32
    )


def row_ids(shape):
    return lax.broadcasted_iota(jnp.int32, shape, 0)


def lane_ids(shape):
    return lax.broadcasted_iota(jnp.int32, shape, 1)


def starts_of(len_ref, shape):
    rows = row_ids(shape)
    start = jnp.zeros(shape, jnp.int32)
    end = jnp.int32(0)
    for k in range(len_ref.shape[1]):
        end = end + len_ref[0, k]
        start = jnp.where(rows >= end, end, start)
    return start


def seen_mask(len_ref, rows):
    shape = (rows, rows)
    lanes = lane_ids(shape)
    return (lanes <= row_ids(shape)) & (lanes >= starts_of(len_ref, shape))


def keep_masks(len_ref, rows, taps):
    shape = (rows, LANES)
    place = row_ids(shape) - starts_of(len_ref, shape)
    return [None] + [(place >= o).astype(f32)[:, :1] for o in range(1, taps)]


def conv(raw, taps, keeps):
    width = len(keeps)
    total = raw * taps[width - 1 : width]
    for o in range(1, width):
        total = total + pltpu.roll(raw, o, 0) * keeps[o] * taps[width - 1 - o : width - o]
    return total


def conv_back(dpre, raw, taps, keeps):
    width = len(keeps)
    rows = raw.shape[0]
    draw = dpre * taps[width - 1 : width]
    dtaps = {width - 1: jnp.sum(dpre * raw, axis=0, keepdims=True)}
    for o in range(1, width):
        kept = dpre * keeps[o]
        draw = draw + pltpu.roll(kept, rows - o, 0) * taps[width - 1 - o : width - o]
        dtaps[width - 1 - o] = jnp.sum(kept * pltpu.roll(raw, o, 0), axis=0, keepdims=True)
    return draw, [dtaps[k] for k in range(width)]


def head_table(channels, head_width):
    shape = (channels, LANES)
    return (row_ids(shape) // head_width == lane_ids(shape)).astype(f32)


def head_spread(channels, head_width):
    shape = (LANES, channels)
    return (lane_ids(shape) // head_width == row_ids(shape)).astype(f32)


def pack_body(bin_ref, slot_ref, co_ref, x_ref, z_ref, bc_ref, dt_ref, dout_ref, a_ref, d_ref):
    rows = dout_ref.shape[0]
    inner = d_ref.shape[0] // rows
    for x in range(inner):
        for z in range(d_ref.shape[1] // LANES):
            low = (z * inner + x) * LANES
            d_ref[x * rows : (x + 1) * rows, z * LANES : (z + 1) * LANES] = dout_ref[
                :, low : low + LANES
            ]
    npan = bin_ref.shape[0]
    channels = x_ref.shape[1]
    heads = dt_ref.shape[1]
    pair = bc_ref.shape[1] // GROUPS
    a_ref[...] = jnp.zeros_like(a_ref)
    group = pl.multiple_of(co_ref[0] * pair, pair)
    shape = (PANEL, LANES)
    low, high = 2 * channels, 2 * channels + pair
    widen = (row_ids((heads, LANES)) == lane_ids((heads, LANES))).astype(bf16)
    wide = dot_nn(dt_ref[...], widen)
    for p in range(npan):
        rows = slice(p * PANEL, (p + 1) * PANEL)
        to = pl.ds(pl.multiple_of(bin_ref[p] * PANEL, PANEL), PANEL)
        a_ref[to, 0:channels] = x_ref[rows, :]
        a_ref[to, channels:low] = z_ref[rows, :]
        a_ref[to, low:high] = bc_ref[rows, pl.ds(group, pair)]
        label = (slot_ref[p] * PANEL + 1 + row_ids(shape)).astype(f32)
        meta = jnp.where(lane_ids(shape) == LANES - 1, label, wide[rows, :])
        a_ref[to, high : high + LANES] = meta.astype(bf16)


def forward_body(
    width,
    heads,
    len_ref,
    co_ref,
    recv_ref,
    cx_ref,
    cbc_ref,
    bias_ref,
    alog_ref,
    skip_ref,
    pt_ref,
    xraw_ref,
    xpre_ref,
    mixed_ref,
    share_ref,
    bcact_ref,
    scores_ref,
    step_ref,
    slope_ref,
    cum_ref,
    cumt_ref,
    zb_ref,
    gated_ref,
):
    rows, channels = xraw_ref.shape
    pair = bcact_ref.shape[1]
    state = pair // 2
    head_width = channels // heads
    base = 2 * channels
    slots = recv_ref.shape[0]
    label = recv_ref[:, base + pair : base + pair + LANES].astype(f32)[:, LANES - 1 :]
    place = (label == (lane_ids((slots, rows)) + 1).astype(f32)).astype(bf16)
    pt_ref[...] = place
    raw = dot_tn(place, recv_ref[...])
    keeps = keep_masks(len_ref, rows, width)
    xraw = raw[:, :channels]
    xraw_ref[...] = xraw.astype(bf16)
    xpre = conv(xraw, cx_ref[...], keeps)
    xpre_ref[...] = xpre
    xact = xpre * jax.nn.sigmoid(xpre)
    bcraw = raw[:, base : base + pair]
    share = share_ref.shape[2] // 2
    for s in range(share_ref.shape[0]):
        tile = bcraw[:, (s // 2) * LANES : (s // 2 + 1) * LANES]
        if s % 2:
            tile = pltpu.roll(tile, share, 1)
        share_ref[s] = jnp.where(lane_ids(tile.shape) < share, tile, 0.0)
    group = pl.multiple_of(co_ref[0] * pair, pair)
    bcpre = conv(bcraw, cbc_ref[:, pl.ds(group, pair)], keeps)
    bcact = (bcpre * jax.nn.sigmoid(bcpre)).astype(bf16)
    bcact_ref[...] = bcact
    scores = dot_nt(bcact[:, state:], bcact[:, :state])
    scores_ref[...] = scores
    mask = seen_mask(len_ref, rows)
    dt = raw[:, base + pair : base + pair + LANES] + bias_ref[...]
    real = lane_ids(dt.shape) < heads
    step = jnp.where(real, jnp.maximum(dt, 0.0) + jnp.log1p(jnp.exp(-jnp.abs(dt))), 0.0)
    step_ref[...] = step
    slope_ref[...] = jnp.where(real, jax.nn.sigmoid(dt), 0.0)
    cum = dot_nn(mask.astype(f32), step * -jnp.exp(alog_ref[...]), exact)
    cum_ref[...] = cum
    cumt = jnp.transpose(cum)[: cumt_ref.shape[0]]
    cumt_ref[...] = cumt
    scaled = (xact * dot_nn(step, head_spread(channels, head_width), exact)).astype(bf16)
    skipped = xact * skip_ref[...]
    low = lane_ids((rows, LANES)) < head_width
    for p in range(channels // LANES):
        tile = scaled[:, p * LANES : (p + 1) * LANES]
        total = skipped[:, p * LANES : (p + 1) * LANES]
        for half in range(2):
            h = 2 * p + half
            gap = jnp.where(mask, cum[:, h : h + 1] - cumt[h : h + 1, :], FAR)
            weights = (scores * jnp.exp(jnp.minimum(gap, 0.0))).astype(bf16)
            part = jnp.where(low if half == 0 else ~low, tile, jnp.zeros_like(tile))
            total = total + dot_nn(weights, part)
        mixed_ref[:, p * LANES : (p + 1) * LANES] = total
    z = raw[:, channels:base]
    zb_ref[...] = z.astype(bf16)
    gated_ref[...] = mixed_ref[...] * (z * jax.nn.sigmoid(z))


def as_column(sums_ref):
    total = sums_ref[:16]
    for k in range(1, sums_ref.shape[0] // 16):
        total = total + sums_ref[16 * k : 16 * (k + 1)]
    eighth = jnp.full((8, LANES), 0.125, f32)
    return dot_tn(total[:8], eighth, exact), dot_tn(total[8:], eighth, exact)


def collect_body(co_ref, *refs):
    blocks, half_ref = refs[:-1], refs[-1]
    count = len(blocks)
    for k, block in enumerate(blocks):
        half_ref[lax.rem(co_ref[1] + count - k, count)] = block[...]


def dnormed_body(co_ref, mine_ref, other_ref, w_ref, p_ref, rows_ref):
    outer = w_ref.shape[0]
    inner = rows_ref.shape[0]
    panel = mine_ref.shape[1] // inner
    w = jnp.concatenate([w_ref[z] for z in range(outer)], axis=1)
    first = co_ref[2] == 0
    count, columns = rows_ref.shape[1:]
    for k in range(inner):
        at = slice(k * panel, (k + 1) * panel)
        mine, other = mine_ref[:, at], other_ref[:, at]
        both = jnp.stack([jnp.where(first, mine, other), jnp.where(first, other, mine)], axis=1)
        rows = both.reshape(count, columns)
        rows_ref[k] = rows
        p_ref[k * count : (k + 1) * count] = dot_nt(rows, w).astype(bf16)


def term_body(scale, rows_ref, normed_ref, term_ref):
    inner, count = rows_ref.shape[:2]
    total = None
    for k in range(inner):
        part = dot_tn(normed_ref[k * count : (k + 1) * count], rows_ref[k])
        total = part if total is None else total + part
    total = (total * scale).astype(bf16)
    channels = total.shape[0]
    for k in range(term_ref.shape[0] // channels):
        term_ref[k * channels : (k + 1) * channels] = total[:, k * LANES : (k + 1) * LANES]


def gather_body(recv_ref, grad_ref):
    count = grad_ref.shape[0]
    total = recv_ref[:count].astype(f32)
    for k in range(1, recv_ref.shape[0] // count):
        total = total + recv_ref[k * count : (k + 1) * count].astype(f32)
    grad_ref[...] = total.astype(bf16)


def cross_body(gated_ref, gain_ref, parts_ref, dnormed_ref, sums_ref):
    gated = gated_ref[...]
    rows = gated.shape[0]
    dnormed = parts_ref[:rows].astype(f32)
    for k in range(1, parts_ref.shape[0] // rows):
        dnormed = dnormed + parts_ref[k * rows : (k + 1) * rows].astype(f32)
    dnormed_ref[...] = dnormed
    ones = jnp.ones((8, gated.shape[1]), f32)
    squares = dot_nt(ones, gated * gated, exact)
    crossing = dot_nt(ones, dnormed * gated * gain_ref[...], exact)
    for k in range(sums_ref.shape[0] // 16):
        sums_ref[16 * k : 16 * k + 8] = squares
        sums_ref[16 * k + 8 : 16 * k + 16] = crossing


def dz_body(
    size,
    dnormed_ref,
    gain_ref,
    gated_ref,
    mixed_ref,
    zb_ref,
    sums_ref,
    normed_ref,
    dgain_ref,
    dy_ref,
    dz_ref,
):
    squares, crossing = as_column(sums_ref)
    inverse = lax.rsqrt(squares / size + 1e-05)
    factor = (inverse * inverse * inverse * crossing / size)[:, :1]
    inverse = inverse[:, :1]
    gain = gain_ref[...]
    gated = gated_ref[...]
    dnormed = dnormed_ref[...]
    scaled = gated * inverse
    normed = (scaled * gain).astype(bf16)
    rows = gated.shape[0]
    for k in range(normed_ref.shape[0] // rows):
        normed_ref[k * rows : (k + 1) * rows] = normed
    dgain_ref[...] = jnp.sum(dnormed * scaled, axis=0, keepdims=True)
    dgated = inverse * (dnormed * gain) - gated * factor
    z = zb_ref[...].astype(f32)
    sig = jax.nn.sigmoid(z)
    dy_ref[...] = dgated * (z * sig)
    dz = dgated * mixed_ref[...] * sig * (1.0 + z * (1.0 - sig))
    dz_ref[...] = dz.astype(bf16)


def backward_body(
    width,
    heads,
    len_ref,
    co_ref,
    dy_ref,
    xpre_ref,
    xraw_ref,
    mixed_ref,
    step_ref,
    slope_ref,
    cum_ref,
    cumt_ref,
    scores_ref,
    bcact_ref,
    cx_ref,
    alog_ref,
    skip_ref,
    gx_ref,
    dcx_ref,
    ddt_ref,
    dheads_ref,
    *refs,
):
    pieces_refs, both_ref = refs[:-1], refs[-1]
    rows, channels = xraw_ref.shape
    pair = bcact_ref.shape[1]
    state = pair // 2
    head_width = channels // heads
    mask = seen_mask(len_ref, rows)
    keeps = keep_masks(len_ref, rows, width)
    xpre = xpre_ref[...]
    sig = jax.nn.sigmoid(xpre)
    xact = xpre * sig
    step = step_ref[...]
    spread = dot_nn(step, head_spread(channels, head_width), exact)
    scaled = (xact * spread).astype(bf16)
    dy = dy_ref[...]
    dyb = dy.astype(bf16)
    cum = cum_ref[...]
    cumt = cumt_ref[...]
    scores = scores_ref[...]
    low = lane_ids((rows, LANES)) < head_width
    dscores = jnp.zeros((rows, rows), f32)
    pieces = []
    for p in range(channels // LANES):
        tile = scaled[:, p * LANES : (p + 1) * LANES]
        dtile = dyb[:, p * LANES : (p + 1) * LANES]
        total = None
        for half in range(2):
            h = 2 * p + half
            gap = jnp.where(mask, cum[:, h : h + 1] - cumt[h : h + 1, :], FAR)
            decay = jnp.exp(jnp.minimum(gap, 0.0))
            weights = (scores * decay).astype(bf16)
            part = jnp.where(low if half == 0 else ~low, dtile, jnp.zeros_like(dtile))
            dscores = dscores + dot_nt(part, tile) * decay
            term = dot_tn(weights, part)
            total = term if total is None else total + term
        pieces.append(total)
    dscaled = jnp.concatenate(pieces, axis=1)
    skip = skip_ref[...]
    table = head_table(channels, head_width)
    inner = mixed_ref[...] - skip * xact
    rowsum = dyb.astype(f32) * inner
    colsum = scaled.astype(f32) * dscaled
    change = dot_nn(rowsum - colsum, table, exact)
    direct = dot_nn(xact * dscaled, table, exact)
    dlog = dot_tn(mask.astype(f32), change, exact)
    rate = -jnp.exp(alog_ref[...])
    ddt = (dlog * rate + direct) * slope_ref[...]
    ddt_ref[...] = ddt
    dskip = dot_nn(
        jnp.broadcast_to(jnp.sum(dy * xact, axis=0, keepdims=True), (8, channels)), table, exact
    )
    dheads_ref[0:1] = jnp.sum(ddt, axis=0, keepdims=True)
    dheads_ref[1:2] = jnp.sum(dlog * step * rate, axis=0, keepdims=True)
    dheads_ref[2:3] = dskip[0:1]
    dpre = (dscaled * spread + skip * dy) * (sig * (1.0 + xpre * (1.0 - sig)))
    draw, dtaps = conv_back(dpre, xraw_ref[...].astype(f32), cx_ref[...], keeps)
    gx_ref[...] = draw.astype(bf16)
    for k in range(width):
        dcx_ref[k : k + 1] = dtaps[k]
    dsb = dscores.astype(bf16)
    dbc = (
        dot_tn(dsb, bcact_ref[:, state:]),
        dot_nn(dsb, bcact_ref[:, :state]),
    )
    share = LANES // 2
    for s in range(len(pieces_refs)):
        low_lane = (s * share) % state
        tile = dbc[s * share // state][:, low_lane // LANES * LANES : (low_lane // LANES + 1) * LANES]
        if low_lane % LANES:
            tile = pltpu.roll(tile, share, 1)
        tile = jnp.where(lane_ids(tile.shape) < share, tile, 0.0)
        both_ref[jnp.bitwise_xor(co_ref[5], s)] = tile.astype(bf16)
    for s, piece_ref in enumerate(pieces_refs):
        piece_ref[...] = both_ref[s]


def share_body(
    width,
    len_ref,
    co_ref,
    share_ref,
    taps_ref,
    gx_ref,
    dz_ref,
    ddt_ref,
    pt_ref,
    dcx_ref,
    dgain_ref,
    dheads_ref,
    *refs,
):
    parts, (back_ref, small_ref) = refs[:-2], refs[-2:]
    rows = ddt_ref.shape[0]
    channels = gx_ref.shape[1]
    slots = back_ref.shape[0]
    keeps = keep_masks(len_ref, rows, width)
    raw = share_ref[co_ref[5]]
    taps = taps_ref[...]
    pre = conv(raw, taps, keeps)
    sig = jax.nn.sigmoid(pre)
    dact = parts[0][...].astype(f32)
    for part in parts[1:]:
        dact = dact + part[...].astype(f32)
    draw, dtaps = conv_back(dact * (sig * (1.0 + pre * (1.0 - sig))), raw, taps, keeps)
    share = LANES // 2
    meta = draw + pltpu.roll(ddt_ref[...], share, 1)
    place = pt_ref[...]
    back_ref[:, :channels] = dot_nn(place, gx_ref[...]).astype(bf16)
    back_ref[:, channels : 2 * channels] = dot_nn(place, dz_ref[...]).astype(bf16)
    last = 2 * channels + LANES
    back_ref[:, 2 * channels : last] = dot_nn(place, meta.astype(bf16)).astype(bf16)
    small_ref[...] = jnp.zeros_like(small_ref)
    small_ref[0:width] = dcx_ref[...]
    small_ref[width : width + 1] = dgain_ref[...]
    small_ref[width + 1 : width + 4, 0:LANES] = dheads_ref[...]
    for k in range(width):
        row = width + 1 + k % 3
        lane = LANES * (1 + k // 3)
        small_ref[row : row + 1, lane : lane + LANES] = dtaps[k]
    half = channels // 2
    block = jnp.concatenate([small_ref[:, :half], small_ref[:, half:]], axis=0).astype(bf16)
    for k in range(slots // PANEL):
        back_ref[k * PANEL : (k + 1) * PANEL, last:] = block


def home_body(
    scale,
    heads,
    bin_ref,
    ret_ref,
    gx_ref,
    gz_ref,
    gbc_ref,
    gdt_ref,
    dcx_ref,
    dcbc_ref,
    dgain_ref,
    dheads_ref,
):
    channels = gx_ref.shape[1]
    width = dcx_ref.shape[0]
    share = gbc_ref.shape[1]
    last = 2 * channels + LANES
    for p in range(bin_ref.shape[0]):
        rows = slice(p * PANEL, (p + 1) * PANEL)
        at = pl.ds(pl.multiple_of(bin_ref[p] * PANEL, PANEL), PANEL)
        gx_ref[rows] = ret_ref[at, :channels]
        gz_ref[rows] = ret_ref[at, channels : 2 * channels]
        meta = ret_ref[at, 2 * channels : last].astype(f32)
        gbc_ref[rows] = meta[:, :share].astype(bf16)
        gdt_ref[rows] = pltpu.roll(meta, LANES - share, 1)[:, :heads].astype(bf16)
    total = None
    for k in range(ret_ref.shape[0] // PANEL):
        part = ret_ref[k * PANEL : (k + 1) * PANEL, last:].astype(f32)
        total = part if total is None else total + part
    total = total * scale
    small = jnp.concatenate([total[:8], total[8:]], axis=1)
    dcx_ref[...] = small[:width]
    dgain_ref[...] = small[width : width + 1]
    dheads_ref[...] = small[width + 1 : width + 4, :heads]
    for k in range(width):
        row = width + 1 + k % 3
        lane = LANES * (1 + k // 3)
        dcbc_ref[k : k + 1] = small[row : row + 1, lane : lane + share]


def per_device(
    x_in,
    z_in,
    bc_in,
    dt_in,
    lengths,
    panel_bin,
    panel_slot,
    conv_x,
    conv_bc,
    dt_bias,
    a_log,
    dskip,
    gain,
    w_out,
    dout,
):
    dp = lax.axis_size("dp")
    tensor = lax.axis_size("tensor")
    inner = DP_INNER
    outer = dp // inner
    t_index = lax.axis_index("tensor")
    x_index = lax.axis_index("dp") % inner
    rows, channels = x_in.shape
    heads = dt_in.shape[1]
    head_width = channels // heads
    width = conv_x.shape[0]
    bc_width = conv_bc.shape[1]
    pair = bc_width // GROUPS
    share = bc_width // tensor
    members = tensor // GROUPS
    group = t_index // members
    local = t_index % members
    slots = dp * PANEL
    size = channels * members
    scale = 1.0 / math.sqrt(rows * dp)
    columns = outer * LANES

    z_index = lax.axis_index("dp") // inner
    coords = jnp.stack(
        [group, t_index // CORES, t_index % CORES, z_index, x_index, local]
    ).astype(jnp.int32)
    over_x = [[z * inner + x for x in range(inner)] for z in range(outer)]
    over_z = [[z * inner + x for z in range(outer)] for x in range(inner)]
    in_group = [[g * members + m for m in range(members)] for g in range(GROUPS)]

    def along_z(block, shift):
        route = [(d, (d + shift * inner) % dp) for d in range(dp)]
        return lax.ppermute(block, "dp", route)

    def along_y(block, shift):
        route = [(t, (t + shift * CORES) % tensor) for t in range(tensor)]
        return lax.ppermute(block, "tensor", route)

    def partner(block, flip):
        return lax.ppermute(block, "tensor", [(t, t ^ flip) for t in range(tensor)])

    def swap(blocks, axis, groups=None):
        return lax.all_to_all(
            blocks, axis, split_axis=0, concat_axis=0, tiled=True, axis_index_groups=groups
        )

    w_cols = lax.all_gather(
        w_out, "dp", axis=0, tiled=True, axis_index_groups=over_z
    ).reshape(outer, channels, LANES)

    send, d_parts = call(
        pack_body,
        [
            shaped((slots, 2 * channels + pair + LANES), bf16),
            shaped((inner * dout.shape[0], columns), bf16),
        ],
        [panel_bin, panel_slot, coords, x_in, z_in, bc_in, dt_in, dout],
        scalars=3,
        moves=True,
        name="pack",
    )
    d_own = swap(d_parts, "dp", over_x)
    send, d_own = lax.optimization_barrier((send, d_own))
    recv = swap(send, "dp")
    ring_y = tensor // CORES
    ups, downs = [d_own], [d_own]
    for step in range(1, ring_y // 2 + 1):
        ups.append(along_y(ups[-1], 1))
        if step < ring_y - ring_y // 2:
            downs.append(along_y(downs[-1], -1))
    blocks = ups + downs[:0:-1]
    blocks[1], w_cols = lax.optimization_barrier((blocks[1], w_cols))
    (mine,) = call(
        collect_body,
        [shaped((ring_y,) + d_own.shape, bf16)],
        [coords] + blocks,
        scalars=1,
        name="collect",
    )
    other = partner(mine, 1)

    bias_row = jnp.pad(dt_bias, (0, LANES - heads))[None, :]
    alog_row = jnp.pad(a_log, (0, LANES - heads))[None, :]
    skip_row = jnp.repeat(dskip, head_width)[None, :]
    gain_row = gain[None, :]
    share_taps = jnp.pad(
        lax.dynamic_slice_in_dim(conv_bc, t_index * share, share, 1),
        ((0, 0), (0, LANES - share)),
    )

    (
        place,
        xraw,
        xpre,
        mixed,
        raw_share,
        bcact,
        scores,
        step,
        slope,
        cum,
        cumt,
        zb,
        gated,
    ) = call(
        functools.partial(forward_body, width, heads),
        [
            shaped((slots, rows), bf16),
            shaped((rows, channels), bf16),
            shaped((rows, channels), f32),
            shaped((rows, channels), f32),
            shaped((members, rows, LANES), f32),
            shaped((rows, pair), bf16),
            shaped((rows, rows), f32),
            shaped((rows, LANES), f32),
            shaped((rows, LANES), f32),
            shaped((rows, LANES), f32),
            shaped((8, rows), f32),
            shaped((rows, channels), bf16),
            shaped((rows, channels), f32),
        ],
        [lengths, coords, recv, conv_x, conv_bc, bias_row, alog_row, skip_row],
        scalars=2,
        cost=4000,
        name="forward",
    )

    partial, out_rows = call(
        dnormed_body,
        [shaped((inner * rows, channels), bf16), shaped((inner, rows, columns), bf16)],
        [coords, mine, other, w_cols],
        scalars=1,
        cost=1200,
        name="dnormed",
    )
    dnormed, sums = call(
        cross_body,
        [shaped((rows, channels), f32), shaped((members * 16, rows), f32)],
        [gated, gain_row, swap(partial, "dp", over_x)],
        cost=500,
        name="cross",
    )
    normed, dgain, dy, dz = call(
        functools.partial(dz_body, size),
        [
            shaped((inner * rows, channels), bf16),
            shaped((1, channels), f32),
            shaped((rows, channels), f32),
            shaped((rows, channels), bf16),
        ],
        [dnormed, gain_row, gated, mixed, zb, swap(sums, "tensor", in_group)],
        cost=1000,
        name="dz",
    )

    gx, dcx, ddt, dheads, *pieces = call(
        functools.partial(backward_body, width, heads),
        [
            shaped((rows, channels), bf16),
            shaped((width, channels), f32),
            shaped((rows, LANES), f32),
            shaped((3, LANES), f32),
        ]
        + [shaped((rows, LANES), bf16)] * members,
        [
            lengths,
            coords,
            dy,
            xpre,
            xraw,
            mixed,
            step,
            slope,
            cum,
            cumt,
            scores,
            bcact,
            conv_x,
            alog_row,
            skip_row,
        ],
        scalars=2,
        cost=6000,
        scratch=[pltpu.VMEM((members, rows, LANES), bf16)],
        name="backward",
    )

    normed_all, gx = lax.optimization_barrier((swap(normed, "dp", over_x), gx))
    (term,) = call(
        functools.partial(term_body, scale),
        [shaped((outer * channels, LANES), bf16)],
        [out_rows, normed_all],
        cost=1200,
        name="term",
    )
    terms = swap(term, "dp", over_z)
    (back,) = call(
        functools.partial(share_body, width),
        [shaped((slots, 2 * channels + LANES + channels // 2), bf16)],
        [
            lengths,
            coords,
            raw_share,
            share_taps,
            gx,
            dz,
            ddt,
            place,
            dcx,
            dgain,
            dheads,
            pieces[0],
        ]
        + [partner(pieces[flip], flip) for flip in range(1, members)],
        scalars=2,
        cost=1500,
        scratch=[pltpu.VMEM((8, channels), f32)],
        name="share",
    )
    back, terms = lax.optimization_barrier((back, terms))
    home = swap(back, "dp")
    (grad_wout,) = call(
        gather_body, [shaped((channels, LANES), bf16)], [terms], name="gather"
    )

    grad_x, grad_z, grad_bc, grad_dt, grad_cx, grad_cbc, grad_gain, grad_heads = call(
        functools.partial(home_body, scale, heads),
        [
            shaped((rows, channels), bf16),
            shaped((rows, channels), bf16),
            shaped((rows, share), bf16),
            shaped((rows, heads), bf16),
            shaped((width, channels), f32),
            shaped((width, share), f32),
            shaped((1, channels), f32),
            shaped((3, heads), f32),
        ],
        [panel_bin, home],
        scalars=1,
        name="home",
    )
    return (
        grad_x,
        grad_z,
        grad_bc,
        grad_dt,
        grad_wout,
        grad_cx,
        grad_cbc,
        grad_gain[0],
        grad_heads,
    )


def solution(mesh):
    placed = (
        P("dp", "tensor"),
        P("dp", "tensor"),
        P("dp", None),
        P("dp", "tensor"),
        P("dp", None),
        P("dp"),
        P("dp"),
        P(None, "tensor"),
        P(),
        P("tensor"),
        P("tensor"),
        P("tensor"),
        P("tensor"),
        P("tensor", "dp"),
        P(("dp", "tensor"), None),
    )
    return jax.shard_map(
        per_device,
        mesh=mesh,
        in_specs=placed,
        out_specs=(
            P("dp", "tensor"),
            P("dp", "tensor"),
            P("dp", "tensor"),
            P("dp", "tensor"),
            P("tensor", "dp"),
            P(None, "tensor"),
            P(None, "tensor"),
            P("tensor"),
            P(None, "tensor"),
        ),
        check_vma=False,
    )
```

```python
import functools
import math

import jax
import jax.numpy as jnp
from jax import lax
from jax.experimental import pallas as pl
from jax.experimental.pallas import tpu as pltpu
from jax.sharding import PartitionSpec as P

GROUPS = 4
DP_INNER = 4
CORES = 2
PANEL = 16
LANES = 128
FAR = -1e30

exact = lax.Precision.HIGHEST
f32 = jnp.float32
bf16 = jnp.bfloat16
smem = pl.BlockSpec(memory_space=pltpu.SMEM)
vmem = pl.BlockSpec(memory_space=pltpu.VMEM)
vmem = pl.BlockSpec(memory_space=pltpu.VMEM)
hbm = pl.BlockSpec(memory_space=pltpu.HBM)


def call(body, outs, ins, scalars=0, moves=False, cost=1, scratch=(), name=None):
    count = len(ins)
    size = sum(math.prod(a.shape) * a.dtype.itemsize for a in list(outs) + list(ins))
    moved = list(ins[scalars:]) + list(outs) if moves else []

    def moving(*refs):
        far, rest = refs[scalars : count + len(outs)], refs[count + len(outs) :]
        held, own, sems = rest[: len(moved)], rest[len(moved) : -1], rest[-1]
        copies = []
        for n in range(len(moved)):
            inward = n < count - scalars
            ends = (far[n], held[n]) if inward else (held[n], far[n])
            copies.append(pltpu.make_async_copy(*ends, sems.at[n]))
        inward, outward = copies[: count - scalars], copies[count - scalars :]
        for copy in inward:
            copy.start()
        for copy in inward:
            copy.wait()
        body(*refs[:scalars], *held, *own)
        for copy in outward:
            copy.start()
        for copy in outward:
            copy.wait()

    place = hbm if moves else vmem
    extra = [pltpu.VMEM(a.shape, a.dtype) for a in moved]
    extra += list(scratch)
    if moves:
        extra.append(pltpu.SemaphoreType.DMA((len(moved),)))
    return pl.pallas_call(
        moving if moves else body,
        out_shape=outs,
        in_specs=[smem] * scalars + [place] * (count - scalars),
        out_specs=[place] * len(outs),
        scratch_shapes=extra,
        compiler_params=pltpu.CompilerParams(vmem_limit_bytes=(58 if moves else 16) << 20),
        cost_estimate=pl.CostEstimate(
            flops=int(cost * 1e6), bytes_accessed=size, transcendentals=0
        ),
        name=name,
    )(*ins)


def shaped(shape, dtype):
    return jax.ShapeDtypeStruct(shape, dtype)


def dot_tn(a, b, precision=None):
    return lax.dot_general(
        a, b, (((0,), (0,)), ((), ())), precision=precision, preferred_element_type=f32
    )


def dot_nt(a, b, precision=None):
    return lax.dot_general(
        a, b, (((1,), (1,)), ((), ())), precision=precision, preferred_element_type=f32
    )


def dot_nn(a, b, precision=None):
    return lax.dot_general(
        a, b, (((1,), (0,)), ((), ())), precision=precision, preferred_element_type=f32
    )


def row_ids(shape):
    return lax.broadcasted_iota(jnp.int32, shape, 0)


def lane_ids(shape):
    return lax.broadcasted_iota(jnp.int32, shape, 1)


def starts_of(len_ref, shape):
    rows = row_ids(shape)
    start = jnp.zeros(shape, jnp.int32)
    end = jnp.int32(0)
    for k in range(len_ref.shape[1]):
        end = end + len_ref[0, k]
        start = jnp.where(rows >= end, end, start)
    return start


def seen_mask(len_ref, rows):
    shape = (rows, rows)
    lanes = lane_ids(shape)
    return (lanes <= row_ids(shape)) & (lanes >= starts_of(len_ref, shape))


def keep_masks(len_ref, rows, taps):
    shape = (rows, LANES)
    place = row_ids(shape) - starts_of(len_ref, shape)
    return [None] + [(place >= o).astype(f32)[:, :1] for o in range(1, taps)]


def conv(raw, taps, keeps):
    width = len(keeps)
    total = raw * taps[width - 1 : width]
    for o in range(1, width):
        total = total + pltpu.roll(raw, o, 0) * keeps[o] * taps[width - 1 - o : width - o]
    return total


def conv_back(dpre, raw, taps, keeps):
    width = len(keeps)
    rows = raw.shape[0]
    draw = dpre * taps[width - 1 : width]
    dtaps = {width - 1: jnp.sum(dpre * raw, axis=0, keepdims=True)}
    for o in range(1, width):
        kept = dpre * keeps[o]
        draw = draw + pltpu.roll(kept, rows - o, 0) * taps[width - 1 - o : width - o]
        dtaps[width - 1 - o] = jnp.sum(kept * pltpu.roll(raw, o, 0), axis=0, keepdims=True)
    return draw, [dtaps[k] for k in range(width)]


def head_table(channels, head_width):
    shape = (channels, LANES)
    return (row_ids(shape) // head_width == lane_ids(shape)).astype(f32)


def head_spread(channels, head_width):
    shape = (LANES, channels)
    return (lane_ids(shape) // head_width == row_ids(shape)).astype(f32)


def pack_body(bin_ref, slot_ref, co_ref, x_ref, z_ref, bc_ref, dt_ref, dout_ref, a_ref, d_ref):
    rows = dout_ref.shape[0]
    inner = d_ref.shape[0] // rows
    for x in range(inner):
        for z in range(d_ref.shape[1] // LANES):
            low = (z * inner + x) * LANES
            d_ref[x * rows : (x + 1) * rows, z * LANES : (z + 1) * LANES] = dout_ref[
                :, low : low + LANES
            ]
    npan = bin_ref.shape[0]
    channels = x_ref.shape[1]
    heads = dt_ref.shape[1]
    pair = bc_ref.shape[1] // GROUPS
    a_ref[...] = jnp.zeros_like(a_ref)
    group = pl.multiple_of(co_ref[0] * pair, pair)
    shape = (PANEL, LANES)
    low, high = 2 * channels, 2 * channels + pair
    widen = (row_ids((heads, LANES)) == lane_ids((heads, LANES))).astype(bf16)
    wide = dot_nn(dt_ref[...], widen)
    for p in range(npan):
        rows = slice(p * PANEL, (p + 1) * PANEL)
        to = pl.ds(pl.multiple_of(bin_ref[p] * PANEL, PANEL), PANEL)
        a_ref[to, 0:channels] = x_ref[rows, :]
        a_ref[to, channels:low] = z_ref[rows, :]
        a_ref[to, low:high] = bc_ref[rows, pl.ds(group, pair)]
        label = (slot_ref[p] * PANEL + 1 + row_ids(shape)).astype(f32)
        meta = jnp.where(lane_ids(shape) == LANES - 1, label, wide[rows, :])
        a_ref[to, high : high + LANES] = meta.astype(bf16)


def forward_body(
    width,
    heads,
    len_ref,
    co_ref,
    recv_ref,
    cx_ref,
    cbc_ref,
    bias_ref,
    alog_ref,
    skip_ref,
    pt_ref,
    xraw_ref,
    xpre_ref,
    mixed_ref,
    share_ref,
    bcact_ref,
    scores_ref,
    step_ref,
    slope_ref,
    cum_ref,
    cumt_ref,
    zb_ref,
    gated_ref,
):
    rows, channels = xraw_ref.shape
    pair = bcact_ref.shape[1]
    state = pair // 2
    head_width = channels // heads
    base = 2 * channels
    slots = recv_ref.shape[0]
    label = recv_ref[:, base + pair : base + pair + LANES].astype(f32)[:, LANES - 1 :]
    place = (label == (lane_ids((slots, rows)) + 1).astype(f32)).astype(bf16)
    pt_ref[...] = place
    raw = dot_tn(place, recv_ref[...])
    keeps = keep_masks(len_ref, rows, width)
    xraw = raw[:, :channels]
    xraw_ref[...] = xraw.astype(bf16)
    xpre = conv(xraw, cx_ref[...], keeps)
    xpre_ref[...] = xpre
    xact = xpre * jax.nn.sigmoid(xpre)
    bcraw = raw[:, base : base + pair]
    share = share_ref.shape[2] // 2
    for s in range(share_ref.shape[0]):
        tile = bcraw[:, (s // 2) * LANES : (s // 2 + 1) * LANES]
        if s % 2:
            tile = pltpu.roll(tile, share, 1)
        share_ref[s] = jnp.where(lane_ids(tile.shape) < share, tile, 0.0)
    group = pl.multiple_of(co_ref[0] * pair, pair)
    bcpre = conv(bcraw, cbc_ref[:, pl.ds(group, pair)], keeps)
    bcact = (bcpre * jax.nn.sigmoid(bcpre)).astype(bf16)
    bcact_ref[...] = bcact
    scores = dot_nt(bcact[:, state:], bcact[:, :state])
    scores_ref[...] = scores
    mask = seen_mask(len_ref, rows)
    dt = raw[:, base + pair : base + pair + LANES] + bias_ref[...]
    real = lane_ids(dt.shape) < heads
    step = jnp.where(real, jnp.maximum(dt, 0.0) + jnp.log1p(jnp.exp(-jnp.abs(dt))), 0.0)
    step_ref[...] = step
    slope_ref[...] = jnp.where(real, jax.nn.sigmoid(dt), 0.0)
    cum = dot_nn(mask.astype(f32), step * -jnp.exp(alog_ref[...]), exact)
    cum_ref[...] = cum
    cumt = jnp.transpose(cum)[: cumt_ref.shape[0]]
    cumt_ref[...] = cumt
    scaled = (xact * dot_nn(step, head_spread(channels, head_width), exact)).astype(bf16)
    skipped = xact * skip_ref[...]
    low = lane_ids((rows, LANES)) < head_width
    for p in range(channels // LANES):
        tile = scaled[:, p * LANES : (p + 1) * LANES]
        total = skipped[:, p * LANES : (p + 1) * LANES]
        for half in range(2):
            h = 2 * p + half
            gap = jnp.where(mask, cum[:, h : h + 1] - cumt[h : h + 1, :], FAR)
            weights = (scores * jnp.exp(jnp.minimum(gap, 0.0))).astype(bf16)
            part = jnp.where(low if half == 0 else ~low, tile, jnp.zeros_like(tile))
            total = total + dot_nn(weights, part)
        mixed_ref[:, p * LANES : (p + 1) * LANES] = total
    z = raw[:, channels:base]
    zb_ref[...] = z.astype(bf16)
    gated_ref[...] = mixed_ref[...] * (z * jax.nn.sigmoid(z))


def as_column(sums_ref):
    total = sums_ref[:16]
    for k in range(1, sums_ref.shape[0] // 16):
        total = total + sums_ref[16 * k : 16 * (k + 1)]
    eighth = jnp.full((8, LANES), 0.125, f32)
    return dot_tn(total[:8], eighth, exact), dot_tn(total[8:], eighth, exact)


def collect_body(co_ref, *refs):
    blocks, half_ref = refs[:-1], refs[-1]
    count = len(blocks)
    for k, block in enumerate(blocks):
        half_ref[lax.rem(co_ref[1] + count - k, count)] = block[...]


def dnormed_body(co_ref, mine_ref, other_ref, w_ref, p_ref, rows_ref):
    outer = w_ref.shape[0]
    inner = rows_ref.shape[0]
    panel = mine_ref.shape[1] // inner
    w = jnp.concatenate([w_ref[z] for z in range(outer)], axis=1)
    first = co_ref[2] == 0
    count, columns = rows_ref.shape[1:]
    for k in range(inner):
        at = slice(k * panel, (k + 1) * panel)
        mine, other = mine_ref[:, at], other_ref[:, at]
        both = jnp.stack([jnp.where(first, mine, other), jnp.where(first, other, mine)], axis=1)
        rows = both.reshape(count, columns)
        rows_ref[k] = rows
        p_ref[k * count : (k + 1) * count] = dot_nt(rows, w).astype(bf16)


def term_body(scale, co_ref, rows_ref, *refs):
    inner = rows_ref.shape[0]
    normed, term_ref = refs[:-1], refs[-1]
    total = None
    for k in range(inner):
        part = dot_tn(normed[k][...], rows_ref[lax.rem(co_ref[4] + inner - k, inner)])
        total = part if total is None else total + part
    total = (total * scale).astype(bf16)
    channels = total.shape[0]
    for k in range(term_ref.shape[0] // channels):
        term_ref[k * channels : (k + 1) * channels] = total[:, k * LANES : (k + 1) * LANES]


def gather_body(recv_ref, grad_ref):
    count = grad_ref.shape[0]
    total = recv_ref[:count].astype(f32)
    for k in range(1, recv_ref.shape[0] // count):
        total = total + recv_ref[k * count : (k + 1) * count].astype(f32)
    grad_ref[...] = total.astype(bf16)


def cross_body(gated_ref, gain_ref, parts_ref, dnormed_ref, sums_ref):
    gated = gated_ref[...]
    rows = gated.shape[0]
    dnormed = parts_ref[:rows].astype(f32)
    for k in range(1, parts_ref.shape[0] // rows):
        dnormed = dnormed + parts_ref[k * rows : (k + 1) * rows].astype(f32)
    dnormed_ref[...] = dnormed
    ones = jnp.ones((8, gated.shape[1]), f32)
    squares = dot_nt(ones, gated * gated, exact)
    crossing = dot_nt(ones, dnormed * gated * gain_ref[...], exact)
    for k in range(sums_ref.shape[0] // 16):
        sums_ref[16 * k : 16 * k + 8] = squares
        sums_ref[16 * k + 8 : 16 * k + 16] = crossing


def dz_body(
    size,
    dnormed_ref,
    gain_ref,
    gated_ref,
    mixed_ref,
    zb_ref,
    sums_ref,
    pt_ref,
    normed_ref,
    dgain_ref,
    dy_ref,
    back_ref,
):
    squares, crossing = as_column(sums_ref)
    inverse = lax.rsqrt(squares / size + 1e-05)
    factor = (inverse * inverse * inverse * crossing / size)[:, :1]
    inverse = inverse[:, :1]
    gain = gain_ref[...]
    gated = gated_ref[...]
    dnormed = dnormed_ref[...]
    scaled = gated * inverse
    normed_ref[...] = (scaled * gain).astype(bf16)
    dgain_ref[...] = jnp.sum(dnormed * scaled, axis=0, keepdims=True)
    dgated = inverse * (dnormed * gain) - gated * factor
    z = zb_ref[...].astype(f32)
    sig = jax.nn.sigmoid(z)
    dy_ref[...] = dgated * (z * sig)
    dz = dgated * mixed_ref[...] * sig * (1.0 + z * (1.0 - sig))
    back_ref[...] = dot_nn(pt_ref[...], dz.astype(bf16)).astype(bf16)


def backward_body(
    width,
    heads,
    len_ref,
    co_ref,
    dy_ref,
    xpre_ref,
    xraw_ref,
    mixed_ref,
    step_ref,
    slope_ref,
    cum_ref,
    cumt_ref,
    scores_ref,
    bcact_ref,
    cx_ref,
    alog_ref,
    skip_ref,
    gx_ref,
    dcx_ref,
    ddt_ref,
    dheads_ref,
    *refs,
):
    pieces_refs, both_ref = refs[:-1], refs[-1]
    rows, channels = xraw_ref.shape
    pair = bcact_ref.shape[1]
    state = pair // 2
    head_width = channels // heads
    mask = seen_mask(len_ref, rows)
    keeps = keep_masks(len_ref, rows, width)
    xpre = xpre_ref[...]
    sig = jax.nn.sigmoid(xpre)
    xact = xpre * sig
    step = step_ref[...]
    spread = dot_nn(step, head_spread(channels, head_width), exact)
    scaled = (xact * spread).astype(bf16)
    dy = dy_ref[...]
    dyb = dy.astype(bf16)
    cum = cum_ref[...]
    cumt = cumt_ref[...]
    scores = scores_ref[...]
    low = lane_ids((rows, LANES)) < head_width
    dscores = jnp.zeros((rows, rows), f32)
    pieces = []
    for p in range(channels // LANES):
        tile = scaled[:, p * LANES : (p + 1) * LANES]
        dtile = dyb[:, p * LANES : (p + 1) * LANES]
        total = None
        for half in range(2):
            h = 2 * p + half
            gap = jnp.where(mask, cum[:, h : h + 1] - cumt[h : h + 1, :], FAR)
            decay = jnp.exp(jnp.minimum(gap, 0.0))
            weights = (scores * decay).astype(bf16)
            part = jnp.where(low if half == 0 else ~low, dtile, jnp.zeros_like(dtile))
            dscores = dscores + dot_nt(part, tile) * decay
            term = dot_tn(weights, part)
            total = term if total is None else total + term
        pieces.append(total)
    dscaled = jnp.concatenate(pieces, axis=1)
    skip = skip_ref[...]
    table = head_table(channels, head_width)
    inner = mixed_ref[...] - skip * xact
    rowsum = dyb.astype(f32) * inner
    colsum = scaled.astype(f32) * dscaled
    change = dot_nn(rowsum - colsum, table, exact)
    direct = dot_nn(xact * dscaled, table, exact)
    dlog = dot_tn(mask.astype(f32), change, exact)
    rate = -jnp.exp(alog_ref[...])
    ddt = (dlog * rate + direct) * slope_ref[...]
    ddt_ref[...] = ddt
    dskip = dot_nn(
        jnp.broadcast_to(jnp.sum(dy * xact, axis=0, keepdims=True), (8, channels)), table, exact
    )
    dheads_ref[0:1] = jnp.sum(ddt, axis=0, keepdims=True)
    dheads_ref[1:2] = jnp.sum(dlog * step * rate, axis=0, keepdims=True)
    dheads_ref[2:3] = dskip[0:1]
    dpre = (dscaled * spread + skip * dy) * (sig * (1.0 + xpre * (1.0 - sig)))
    draw, dtaps = conv_back(dpre, xraw_ref[...].astype(f32), cx_ref[...], keeps)
    gx_ref[...] = draw.astype(bf16)
    for k in range(width):
        dcx_ref[k : k + 1] = dtaps[k]
    dsb = dscores.astype(bf16)
    dbc = (
        dot_tn(dsb, bcact_ref[:, state:]),
        dot_nn(dsb, bcact_ref[:, :state]),
    )
    share = LANES // 2
    for s in range(len(pieces_refs)):
        low_lane = (s * share) % state
        tile = dbc[s * share // state][:, low_lane // LANES * LANES : (low_lane // LANES + 1) * LANES]
        if low_lane % LANES:
            tile = pltpu.roll(tile, share, 1)
        tile = jnp.where(lane_ids(tile.shape) < share, tile, 0.0)
        both_ref[jnp.bitwise_xor(co_ref[5], s)] = tile.astype(bf16)
    for s, piece_ref in enumerate(pieces_refs):
        piece_ref[...] = both_ref[s]


def share_body(
    width,
    len_ref,
    co_ref,
    share_ref,
    taps_ref,
    gx_ref,
    ddt_ref,
    pt_ref,
    dcx_ref,
    dgain_ref,
    dheads_ref,
    *refs,
):
    parts, (back_ref, small_ref) = refs[:-2], refs[-2:]
    rows = ddt_ref.shape[0]
    channels = gx_ref.shape[1]
    slots = back_ref.shape[0]
    keeps = keep_masks(len_ref, rows, width)
    raw = share_ref[co_ref[5]]
    taps = taps_ref[...]
    pre = conv(raw, taps, keeps)
    sig = jax.nn.sigmoid(pre)
    dact = parts[0][...].astype(f32)
    for part in parts[1:]:
        dact = dact + part[...].astype(f32)
    draw, dtaps = conv_back(dact * (sig * (1.0 + pre * (1.0 - sig))), raw, taps, keeps)
    share = LANES // 2
    meta = draw + pltpu.roll(ddt_ref[...], share, 1)
    place = pt_ref[...]
    back_ref[:, :channels] = dot_nn(place, gx_ref[...]).astype(bf16)
    last = channels + LANES
    back_ref[:, channels : last] = dot_nn(place, meta.astype(bf16)).astype(bf16)
    small_ref[...] = jnp.zeros_like(small_ref)
    small_ref[0:width] = dcx_ref[...]
    small_ref[width : width + 1] = dgain_ref[...]
    small_ref[width + 1 : width + 4, 0:LANES] = dheads_ref[...]
    for k in range(width):
        row = width + 1 + k % 3
        lane = LANES * (1 + k // 3)
        small_ref[row : row + 1, lane : lane + LANES] = dtaps[k]
    half = channels // 2
    block = jnp.concatenate([small_ref[:, :half], small_ref[:, half:]], axis=0).astype(bf16)
    for k in range(slots // PANEL):
        back_ref[k * PANEL : (k + 1) * PANEL, last:] = block


def home_z_body(bin_ref, ret_ref, gz_ref):
    for p in range(bin_ref.shape[0]):
        at = pl.ds(pl.multiple_of(bin_ref[p] * PANEL, PANEL), PANEL)
        gz_ref[p * PANEL : (p + 1) * PANEL] = ret_ref[at]


def home_body(
    scale,
    heads,
    bin_ref,
    ret_ref,
    gx_ref,
    gbc_ref,
    gdt_ref,
    dcx_ref,
    dcbc_ref,
    dgain_ref,
    dheads_ref,
):
    channels = gx_ref.shape[1]
    width = dcx_ref.shape[0]
    share = gbc_ref.shape[1]
    last = channels + LANES
    for p in range(bin_ref.shape[0]):
        rows = slice(p * PANEL, (p + 1) * PANEL)
        at = pl.ds(pl.multiple_of(bin_ref[p] * PANEL, PANEL), PANEL)
        gx_ref[rows] = ret_ref[at, :channels]
        meta = ret_ref[at, channels:last].astype(f32)
        gbc_ref[rows] = meta[:, :share].astype(bf16)
        gdt_ref[rows] = pltpu.roll(meta, LANES - share, 1)[:, :heads].astype(bf16)
    total = None
    for k in range(ret_ref.shape[0] // PANEL):
        part = ret_ref[k * PANEL : (k + 1) * PANEL, last:].astype(f32)
        total = part if total is None else total + part
    total = total * scale
    small = jnp.concatenate([total[:8], total[8:]], axis=1)
    dcx_ref[...] = small[:width]
    dgain_ref[...] = small[width : width + 1]
    dheads_ref[...] = small[width + 1 : width + 4, :heads]
    for k in range(width):
        row = width + 1 + k % 3
        lane = LANES * (1 + k // 3)
        dcbc_ref[k : k + 1] = small[row : row + 1, lane : lane + share]


def per_device(
    x_in,
    z_in,
    bc_in,
    dt_in,
    lengths,
    panel_bin,
    panel_slot,
    conv_x,
    conv_bc,
    dt_bias,
    a_log,
    dskip,
    gain,
    w_out,
    dout,
):
    dp = lax.axis_size("dp")
    tensor = lax.axis_size("tensor")
    inner = DP_INNER
    outer = dp // inner
    t_index = lax.axis_index("tensor")
    x_index = lax.axis_index("dp") % inner
    rows, channels = x_in.shape
    heads = dt_in.shape[1]
    head_width = channels // heads
    width = conv_x.shape[0]
    bc_width = conv_bc.shape[1]
    pair = bc_width // GROUPS
    share = bc_width // tensor
    members = tensor // GROUPS
    group = t_index // members
    local = t_index % members
    slots = dp * PANEL
    size = channels * members
    scale = 1.0 / math.sqrt(rows * dp)
    columns = outer * LANES

    z_index = lax.axis_index("dp") // inner
    coords = jnp.stack(
        [group, t_index // CORES, t_index % CORES, z_index, x_index, local]
    ).astype(jnp.int32)
    over_x = [[z * inner + x for x in range(inner)] for z in range(outer)]
    over_z = [[z * inner + x for z in range(outer)] for x in range(inner)]
    in_group = [[g * members + m for m in range(members)] for g in range(GROUPS)]

    def along_z(block, shift):
        route = [(d, (d + shift * inner) % dp) for d in range(dp)]
        return lax.ppermute(block, "dp", route)

    def along_x(block, shift):
        route = []
        for z in range(outer):
            for x in range(inner):
                route.append((z * inner + x, z * inner + (x + shift) % inner))
        return lax.ppermute(block, "dp", route)

    def along_y(block, shift):
        route = [(t, (t + shift * CORES) % tensor) for t in range(tensor)]
        return lax.ppermute(block, "tensor", route)

    def partner(block, flip):
        return lax.ppermute(block, "tensor", [(t, t ^ flip) for t in range(tensor)])

    def swap(blocks, axis, groups=None):
        return lax.all_to_all(
            blocks, axis, split_axis=0, concat_axis=0, tiled=True, axis_index_groups=groups
        )

    w_cols = lax.all_gather(
        w_out, "dp", axis=0, tiled=True, axis_index_groups=over_z
    ).reshape(outer, channels, LANES)

    send, d_parts = call(
        pack_body,
        [
            shaped((slots, 2 * channels + pair + LANES), bf16),
            shaped((inner * dout.shape[0], columns), bf16),
        ],
        [panel_bin, panel_slot, coords, x_in, z_in, bc_in, dt_in, dout],
        scalars=3,
        moves=True,
        name="pack",
    )
    d_own = swap(d_parts, "dp", over_x)
    send, d_own = lax.optimization_barrier((send, d_own))
    recv = swap(send, "dp")
    ring_y = tensor // CORES
    ups, downs = [d_own], [d_own]
    for step in range(1, ring_y // 2 + 1):
        ups.append(along_y(ups[-1], 1))
        if step < ring_y - ring_y // 2:
            downs.append(along_y(downs[-1], -1))
    blocks = ups + downs[:0:-1]
    blocks[1], w_cols = lax.optimization_barrier((blocks[1], w_cols))
    (mine,) = call(
        collect_body,
        [shaped((ring_y,) + d_own.shape, bf16)],
        [coords] + blocks,
        scalars=1,
        name="collect",
    )
    other = partner(mine, 1)

    bias_row = jnp.pad(dt_bias, (0, LANES - heads))[None, :]
    alog_row = jnp.pad(a_log, (0, LANES - heads))[None, :]
    skip_row = jnp.repeat(dskip, head_width)[None, :]
    gain_row = gain[None, :]
    share_taps = jnp.pad(
        lax.dynamic_slice_in_dim(conv_bc, t_index * share, share, 1),
        ((0, 0), (0, LANES - share)),
    )

    (
        place,
        xraw,
        xpre,
        mixed,
        raw_share,
        bcact,
        scores,
        step,
        slope,
        cum,
        cumt,
        zb,
        gated,
    ) = call(
        functools.partial(forward_body, width, heads),
        [
            shaped((slots, rows), bf16),
            shaped((rows, channels), bf16),
            shaped((rows, channels), f32),
            shaped((rows, channels), f32),
            shaped((members, rows, LANES), f32),
            shaped((rows, pair), bf16),
            shaped((rows, rows), f32),
            shaped((rows, LANES), f32),
            shaped((rows, LANES), f32),
            shaped((rows, LANES), f32),
            shaped((8, rows), f32),
            shaped((rows, channels), bf16),
            shaped((rows, channels), f32),
        ],
        [lengths, coords, recv, conv_x, conv_bc, bias_row, alog_row, skip_row],
        scalars=2,
        cost=4000,
        name="forward",
    )

    partial, out_rows = call(
        dnormed_body,
        [shaped((inner * rows, channels), bf16), shaped((inner, rows, columns), bf16)],
        [coords, mine, other, w_cols],
        scalars=1,
        cost=1200,
        name="dnormed",
    )
    dnormed, sums = call(
        cross_body,
        [shaped((rows, channels), f32), shaped((members * 16, rows), f32)],
        [gated, gain_row, swap(partial, "dp", over_x)],
        cost=500,
        name="cross",
    )
    normed, dgain, dy, back_z = call(
        functools.partial(dz_body, size),
        [
            shaped((rows, channels), bf16),
            shaped((1, channels), f32),
            shaped((rows, channels), f32),
            shaped((slots, channels), bf16),
        ],
        [dnormed, gain_row, gated, mixed, zb, swap(sums, "tensor", in_group), place],
        cost=1000,
        name="dz",
    )

    home_z = swap(back_z, "dp")
    normed_all = [normed] + [along_x(normed, k) for k in range(1, inner)]
    gx, dcx, ddt, dheads, *pieces = call(
        functools.partial(backward_body, width, heads),
        [
            shaped((rows, channels), bf16),
            shaped((width, channels), f32),
            shaped((rows, LANES), f32),
            shaped((3, LANES), f32),
        ]
        + [shaped((rows, LANES), bf16)] * members,
        [
            lengths,
            coords,
            dy,
            xpre,
            xraw,
            mixed,
            step,
            slope,
            cum,
            cumt,
            scores,
            bcact,
            conv_x,
            alog_row,
            skip_row,
        ],
        scalars=2,
        cost=6000,
        scratch=[pltpu.VMEM((members, rows, LANES), bf16)],
        name="backward",
    )

    normed_all, gx = lax.optimization_barrier((normed_all, gx))
    (term,) = call(
        functools.partial(term_body, scale),
        [shaped((outer * channels, LANES), bf16)],
        [coords, out_rows] + normed_all,
        scalars=1,
        cost=1200,
        name="term",
    )
    term, home_z = lax.optimization_barrier((term, home_z))
    terms = swap(term, "dp", over_z)
    (back,) = call(
        functools.partial(share_body, width),
        [shaped((slots, channels + LANES + channels // 2), bf16)],
        [
            lengths,
            coords,
            raw_share,
            share_taps,
            gx,
            ddt,
            place,
            dcx,
            dgain,
            dheads,
            pieces[0],
        ]
        + [partner(pieces[flip], flip) for flip in range(1, members)],
        scalars=2,
        cost=1500,
        scratch=[pltpu.VMEM((8, channels), f32)],
        name="share",
    )
    back, terms = lax.optimization_barrier((back, terms))
    home = swap(back, "dp")
    (grad_wout,) = call(
        gather_body, [shaped((channels, LANES), bf16)], [terms], name="gather"
    )

    (grad_z,) = call(
        home_z_body,
        [shaped((rows, channels), bf16)],
        [panel_bin, home_z],
        scalars=1,
        name="home_z",
    )
    grad_x, grad_bc, grad_dt, grad_cx, grad_cbc, grad_gain, grad_heads = call(
        functools.partial(home_body, scale, heads),
        [
            shaped((rows, channels), bf16),
            shaped((rows, share), bf16),
            shaped((rows, heads), bf16),
            shaped((width, channels), f32),
            shaped((width, share), f32),
            shaped((1, channels), f32),
            shaped((3, heads), f32),
        ],
        [panel_bin, home],
        scalars=1,
        name="home",
    )
    return (
        grad_x,
        grad_z,
        grad_bc,
        grad_dt,
        grad_wout,
        grad_cx,
        grad_cbc,
        grad_gain[0],
        grad_heads,
    )


def solution(mesh):
    placed = (
        P("dp", "tensor"),
        P("dp", "tensor"),
        P("dp", None),
        P("dp", "tensor"),
        P("dp", None),
        P("dp"),
        P("dp"),
        P(None, "tensor"),
        P(),
        P("tensor"),
        P("tensor"),
        P("tensor"),
        P("tensor"),
        P("tensor", "dp"),
        P(("dp", "tensor"), None),
    )
    return jax.shard_map(
        per_device,
        mesh=mesh,
        in_specs=placed,
        out_specs=(
            P("dp", "tensor"),
            P("dp", "tensor"),
            P("dp", "tensor"),
            P("dp", "tensor"),
            P("tensor", "dp"),
            P(None, "tensor"),
            P(None, "tensor"),
            P("tensor"),
            P(None, "tensor"),
        ),
        check_vma=False,
    )
```
